256 devices in a mesh: grp: 8 (over z), col: 32 (over x, y, core).
Axes of the slice: x: 4, y: 4, z: 8, core: 2. Of those that a mesh axis runs over, the one named last changes fastest.
Arguments:
- coeff: bfloat16 [8192, 3, 128, 128], P(('grp', 'col')), may hold values from -0.09375 to 0.09375
- scaling: bfloat16 [8192, 128], P(('grp', 'col')), may hold values from 0.049804688 to 20
- block_rows: int32 [8192, 3], P(('grp', 'col')), may hold values from 0 to 2047, as said below
- precond: float32 [2048, 128, 128], P(('grp', 'col')), may hold values from -1 to 8, as said below
- rhs: float32 [2048, 128], P(('grp', 'col')), may hold values from -6 to 6
Outputs:
- normal_blocks: float32 [2048, 7, 128, 128], P(('grp', 'col'))
- solution: float32 [2048, 128], P(('grp', 'col'))
- residual: float32 [2048, 128], P(('grp', 'col'))
The draws below stay inside these ranges and needn't reach their ends.
Inputs may be any that keep to these rules, and one draw needn't show every extreme that they name: For column block j held by a device of grp group g, block_rows[j, 0] = h lies among the 256 block rows of group g, and block_rows[j, 1], block_rows[j, 2] are h moved by 8 and 24 block rows, cyclically within those 256 rows. Of the 32 column blocks of one device, at most 1 have block_rows[j, 0] among the rows of any one device, and some device's rows hold exactly 1 of them. `precond`: each block is symmetric and positive definite.
All inputs are finite; a program needn't handle non-finite values.
Results may differ from the reference program's by a relative error of at most 0.0003.
Values may be sent and summed in bfloat16 or wider, within the bound.
A program may use at most 128 MiB of HBM per device.

```python
import math
import jax
import jax.numpy as jnp
from jax import lax

BS = 128
RB_DEV = 8
CB_DEV = 32
ITERS = 2
ROW_BLOCKS = 2048
COL_BLOCKS = 8192
N_COL = 32
DEVICES = 256


def draw_block_rows(key, part):
    key = jax.random.fold_in(key, 11)
    perm_keys = jax.random.split(jax.random.fold_in(key, 1), DEVICES)
    orders = jax.vmap(lambda single: jax.random.permutation(single, N_COL))(perm_keys)
    columns = jnp.arange(CB_DEV) % N_COL
    home_dev = orders[:, columns]
    local_row = jax.random.randint(jax.random.fold_in(key, 2), (DEVICES, CB_DEV), 0, RB_DEV)
    group_rows = RB_DEV * N_COL
    group_start = (jnp.arange(DEVICES) // N_COL)[:, None] * group_rows
    home_row = home_dev * RB_DEV + local_row
    row_list = [group_start + (home_row + lift_by * RB_DEV) % group_rows for lift_by in (0, 1, 3)]
    return jnp.stack(row_list, axis=-1).reshape(COL_BLOCKS, 3).astype(jnp.int32)


def draw_precond(key, part):
    key = jax.random.fold_in(key, 7)
    noise = jax.random.uniform(jax.random.fold_in(key, 1), (ROW_BLOCKS, BS, BS), jnp.float32, -1.0, 1.0)
    symmetric = (noise + jnp.swapaxes(noise, 1, 2)) * (0.4 / BS)
    diagonal = jax.random.uniform(jax.random.fold_in(key, 2), (ROW_BLOCKS, BS), jnp.float32, 1.0, 2.0)
    row_scale = jnp.ones((ROW_BLOCKS, BS), jnp.float32)
    core = symmetric + jnp.eye(BS, dtype=jnp.float32)[None] * diagonal[:, None, :]
    return (0.5 * row_scale[:, :, None] * core).astype(jnp.float32)


def steps_of(own_key, extent, cuts, least, top_value):
    gain = 1.0
    for axis_at, blocks in cuts:
        heights = jax.random.uniform(jax.random.fold_in(jax.random.fold_in(own_key, 6), axis_at), (blocks,), jnp.float32, least / len(cuts), top_value / len(cuts))
        gain = gain * jnp.repeat(jnp.exp(heights), extent[axis_at] // blocks).reshape((-1,) + (1,) * (len(extent) - 1 - axis_at))
    return gain


def bell_draw(stream_key, extent, width, most, cuts=(), held_as=jnp.bfloat16):
    values = jax.random.normal(stream_key, extent, jnp.float32) * width
    if len(cuts) > 0:
        values = steps_of(stream_key, extent, cuts, -0.22, 0.18) * values
    return jnp.clip(values, min=-most, max=most).astype(held_as)


def setup_inputs(seed: int = 0) -> dict:
    splits = jax.random.split(jax.random.key(seed), 6)
    coeff = bell_draw(splits[0], (COL_BLOCKS, 3, BS, BS), (30 * BS) ** -0.5, 0.09375, ((0, 256),))
    scaling = jnp.clip(jnp.exp(math.log(20.0) - 5.9953784 * jax.random.uniform(splits[1], (COL_BLOCKS, BS), jnp.float32) ** steps_of(splits[1], (COL_BLOCKS, BS), ((0, 256),), -0.2, 0.2)), 0.049804688, 20.0).astype(jnp.bfloat16)
    block_rows = draw_block_rows(jax.random.fold_in(splits[5], 71), 0)
    precond = draw_precond(jax.random.fold_in(splits[5], 71), 0)
    rhs = bell_draw(splits[4], (ROW_BLOCKS, BS), 1.0, 6.0, ((0, 256),), jnp.float32)
    return dict(coeff=coeff, scaling=scaling, block_rows=block_rows, precond=precond, rhs=rhs)


OFFSETS = (0, 1, 3)
SHIFTS = (0, 1, -1, 2, -2, 3, -3)
REGULAR = 0.5
HIGHEST = lax.Precision.HIGHEST


def slot_of(leader, partner):
    return SHIFTS.index(OFFSETS[partner] - OFFSETS[leader])


def assemble(coeff, scaling, block_rows):
    shaped_coeff = coeff.reshape(DEVICES, CB_DEV, 3, BS, BS)
    shaped_scale = scaling.reshape(DEVICES, CB_DEV, BS)
    shaped_rows = block_rows.reshape(DEVICES, CB_DEV, 3)

    def add_device(normal, pieces):
        blocks, weights, rows_here = pieces
        full_blocks = blocks.astype(jnp.float32)
        scaled = full_blocks * weights.astype(jnp.float32)[:, None, None, :]
        products = jnp.einsum("jkac,jlbc->jklab", scaled, full_blocks, precision=HIGHEST)
        for leader in range(3):
            for partner in range(3):
                normal = normal.at[rows_here[:, leader], slot_of(leader, partner)].add(products[:, leader, partner])
        return normal, None

    normal = jnp.zeros((ROW_BLOCKS, 7, BS, BS), jnp.float32)
    normal, unused = lax.scan(add_device, normal, (shaped_coeff, shaped_scale, shaped_rows))
    return normal.at[:, 0].add(REGULAR * jnp.eye(BS, dtype=jnp.float32))


def neighbour_index():
    position = jnp.arange(ROW_BLOCKS, dtype=jnp.int32)
    group_rows = RB_DEV * N_COL
    group_start = (position // group_rows) * group_rows
    inside = position % group_rows
    row_moves = jnp.array(SHIFTS, dtype=jnp.int32) * RB_DEV
    return (group_start[:, None] + (inside[:, None] + row_moves[None, :]) % group_rows).astype(jnp.int32)


def apply_normal(normal, vector, neighbours):
    return jnp.einsum("qoab,qob->qa", normal, vector[neighbours], precision=HIGHEST)


def precondition(precond, vector):
    return jnp.einsum("qab,qb->qa", precond, vector, precision=HIGHEST)


def reference(coeff, scaling, block_rows, precond, rhs):
    normal = assemble(coeff, scaling, block_rows)
    neighbours = neighbour_index()
    solution = jnp.zeros_like(rhs)
    residual = rhs
    search = precondition(precond, residual)
    norm_now = jnp.sum(residual * search)
    for sweep in range(ITERS):
        mapped = apply_normal(normal, search, neighbours)
        step_length = norm_now / jnp.sum(search * mapped)
        solution = solution + step_length * search
        residual = residual - step_length * mapped
        smoothed = precondition(precond, residual)
        norm_next = jnp.sum(residual * smoothed)
        search = smoothed + (norm_next / norm_now) * search
        norm_now = norm_next
    return normal, solution, residual
```

```python
import jax
import jax.numpy as jnp
from jax import lax
from jax.experimental import pallas as pl
from jax.experimental.pallas import tpu as pltpu
from jax.sharding import PartitionSpec as P

MESH = pl.DeviceIdType.MESH
RING = 32
ROWS = 8
BS = 128
WIDE = 3 * BS
LAYERS = 8
BATCH = 4
REGULAR = 0.5
LEVELS = 32767.0

_GROUPS = (
    ((1, 0), (3, 0), (0, 1), (0, 3)),
    ((2, 0), (0, 2)),
    ((1, 1), (3, 3)),
    ((1, 3), (3, 1)),
    ((2, 1), (2, 3), (1, 2), (3, 2)),
    ((2, 2),),
)
MOVES = [(0, 0, 0), (0, 0, 1)] + [
    (dx, dy, dc) for group in _GROUPS for dc in (0, 1) for dx, dy in group
]


def moved(me, move):
    dx, dy, dc = move
    return (
        lax.rem(me // 8 + dx, 4) * 8
        + lax.rem(lax.rem(me // 2, 4) + dy, 4) * 2
        + lax.rem(me + dc, 2)
    )


def on_col(index):
    return {"col": index}


def spread(columns, first, out, lead):
    out[lead] = jnp.broadcast_to(columns[:, first : first + 1], (BS, BS))


def kernel(
    coeff_hbm,
    scaling_ref,
    rows_ref,
    precond_hbm,
    rhs_ref,
    normal_hbm,
    solution_ref,
    residual_ref,
    coeff,
    scale32,
    pick,
    stage,
    stage_meta,
    arrived,
    arrived_meta,
    products,
    total,
    precond,
    wide,
    wide_own,
    halo,
    part,
    part_in,
    codes,
    codes_in,
    steps,
    steps_in,
    normal,
    red_a,
    red_b,
    red_c,
    load_sem,
    send_sem,
    recv_sem,
    meta_send,
    meta_recv,
    halo_send,
    halo_recv,
    part_send,
    part_recv,
    code_send,
    code_recv,
    step_send,
    step_recv,
    red_send,
    red_recv,
    out_sem,
):
    me = lax.axis_index("col")
    layer = lax.axis_index("grp")
    before, after = lax.rem(me + RING - 1, RING), lax.rem(me + 1, RING)
    ahead, behind = lax.rem(me + 2, RING), lax.rem(me + RING - 2, RING)
    peers = [moved(me, move) for move in MOVES]

    load = pltpu.make_async_copy(coeff_hbm, coeff, load_sem.at[0])
    load.start()
    load_precond = pltpu.make_async_copy(precond_hbm, precond, load_sem.at[1])
    load_precond.start()

    barrier = pltpu.get_barrier_semaphore()
    for peer in peers[1:]:
        pl.semaphore_signal(barrier, inc=1, device_id=on_col(peer), device_id_type=MESH)
    for other in range(1, LAYERS):
        pl.semaphore_signal(
            barrier, inc=1, device_id={"grp": layer ^ other}, device_id_type=MESH
        )

    scale32[...] = scaling_ref[...].astype(jnp.float32)
    first_row = layer * (RING * ROWS)
    for slot in range(RING):
        home = lax.rem(peers[slot] + RING - 1, RING) * ROWS + first_row
        found = jnp.int32(0)
        for j in range(RING):
            local = rows_ref[j, 0] - home
            found = jnp.where((local >= 0) & (local < ROWS), j * ROWS + local, found)
        pick[slot] = found

    load.wait()
    pl.semaphore_wait(barrier, RING - 1 + LAYERS - 1)

    def place(slot, blocks, meta):
        found = pick[slot]
        source = found // ROWS
        blocks[slot] = coeff[source]
        meta[slot, 0:1] = scale32[pl.ds(source, 1), :]
        meta[slot, 1:2] = jnp.full((1, BS), lax.rem(found, ROWS), jnp.int32).astype(jnp.float32)

    sends = []
    for slot in range(1, RING):
        place(slot, stage, stage_meta)
        for source, target, out, into in (
            (stage_meta, arrived_meta, meta_send, meta_recv),
            (stage, arrived, send_sem, recv_sem),
        ):
            copy = pltpu.make_async_remote_copy(
                src_ref=source.at[slot],
                dst_ref=target.at[slot],
                send_sem=out.at[slot],
                recv_sem=into.at[slot],
                device_id=on_col(peers[slot]),
                device_id_type=MESH,
            )
            copy.start()
            sends.append(copy)
    place(0, arrived, arrived_meta)

    def transposed(pieces):
        rows = [*pieces, jnp.zeros((BS - ROWS * len(pieces), BS), jnp.float32)]
        return jnp.transpose(jnp.concatenate(rows, axis=0))

    def apply_precond(vector):
        columns = transposed([vector])
        for row in range(ROWS):
            spread(columns, row, wide_own, row)
        outs = []
        for row in range(ROWS):
            acc = jnp.zeros((8, BS), jnp.float32)
            for chunk in range(0, BS, 8):
                acc += precond[row, chunk : chunk + 8, :] * wide_own[row, chunk : chunk + 8, :]
            outs.append(jnp.sum(acc, axis=0, keepdims=True))
        return jnp.concatenate(outs, axis=0)

    def send_halo(turn, vector):
        halo[turn, 0] = vector
        copies = []
        for way, peer in ((1, after), (2, behind)):
            copy = pltpu.make_async_remote_copy(
                src_ref=halo.at[turn, 0],
                dst_ref=halo.at[turn, way],
                send_sem=halo_send.at[turn, way],
                recv_sem=halo_recv.at[turn, way],
                device_id=on_col(peer),
                device_id_type=MESH,
            )
            copy.start()
            copies.append(copy)
        return copies

    def apply_normal(turn):
        columns = transposed([halo[turn, 1], halo[turn, 0], halo[turn, 2]])
        for row in range(ROWS):
            for k in range(3):
                wide[row, k * BS : (k + 1) * BS, :] = jnp.broadcast_to(
                    columns[:, k * ROWS + row : k * ROWS + row + 1], (BS, BS)
                )

        def one(row, carry):
            acc = [jnp.zeros((8, BS), jnp.float32) for _ in range(3)]
            for chunk in range(0, WIDE, 8):
                v = wide[row, chunk : chunk + 8, :]
                for k in range(3):
                    acc[k] += total[row, chunk : chunk + 8, k * BS : (k + 1) * BS] * v
            for k in range(3):
                part[turn, k, pl.ds(row, 1), :] = jnp.sum(acc[k], axis=0, keepdims=True)
            return carry

        lax.fori_loop(0, ROWS, one, 0)

    def send_part(turn):
        copies = []
        for k, way, peer in ((0, 0, before), (2, 1, ahead)):
            copy = pltpu.make_async_remote_copy(
                src_ref=part.at[turn, k],
                dst_ref=part_in.at[turn, way],
                send_sem=part_send.at[turn, way],
                recv_sem=part_recv.at[turn, way],
                device_id=on_col(peer),
                device_id_type=MESH,
            )
            copy.start()
            copies.append(copy)
        return copies

    def all_sum(turn, values):
        rows = [jnp.sum(v, axis=0, keepdims=True) for v in values]
        rows.append(jnp.zeros((8 - len(rows), BS), jnp.float32))
        value = jnp.concatenate(rows, axis=0)
        base = 0
        for buffer, count, target in (
            (red_a, 8, lambda t: {"col": me ^ t}),
            (red_b, 4, lambda t: {"col": me ^ (8 * t)}),
            (red_c, 8, lambda t: {"grp": layer ^ t}),
        ):
            buffer[turn, 0] = value
            copies = []
            for t in range(1, count):
                copy = pltpu.make_async_remote_copy(
                    src_ref=buffer.at[turn, 0],
                    dst_ref=buffer.at[turn, t],
                    send_sem=red_send.at[turn, base + t],
                    recv_sem=red_recv.at[turn, base + t],
                    device_id=target(t),
                    device_id_type=MESH,
                )
                copy.start()
                copies.append(copy)
            for copy in copies:
                copy.wait()
            value = jnp.sum(buffer[turn], axis=0)
            base += count
        sums = jnp.sum(value, axis=1, keepdims=True)
        return [sums[i : i + 1, :] for i in range(len(values))]

    load_precond.wait()
    rhs = rhs_ref[...]
    smooth0 = apply_precond(rhs)
    halo_copies = send_halo(0, smooth0)

    def batch(number, carry):
        for i in range(BATCH):
            slot = number * BATCH + i

            @pl.when(slot > 0)
            def _():
                for source, target, out, into in (
                    (stage_meta, arrived_meta, meta_send, meta_recv),
                    (stage, arrived, send_sem, recv_sem),
                ):
                    pltpu.make_async_remote_copy(
                        src_ref=source.at[slot],
                        dst_ref=target.at[slot],
                        send_sem=out.at[slot],
                        recv_sem=into.at[slot],
                        device_id=on_col(after),
                        device_id_type=MESH,
                    ).wait_recv()

            blocks = arrived[slot].reshape(WIDE, BS)
            scaled = blocks.astype(jnp.float32) * arrived_meta[slot, 0:1]
            high = scaled.astype(jnp.bfloat16)
            low = (scaled - high.astype(jnp.float32)).astype(jnp.bfloat16)
            products[i] = lax.dot_general(
                jnp.concatenate([high, low], axis=1),
                jnp.concatenate([blocks, blocks], axis=1),
                (((1,), (1,)), ((), ())),
                preferred_element_type=jnp.float32,
            )
        rows_at = [
            jnp.broadcast_to(arrived_meta[number * BATCH + i, 1:2], (8, BS)) for i in range(BATCH)
        ]
        masks = [
            [jnp.where(at == float(row), 1.0, 0.0) for at in rows_at] for row in range(ROWS)
        ]

        def add(chunk, inner):
            at = pl.ds(pl.multiple_of(chunk * 8, 8), 8)
            for k in range(3):
                lanes = slice(k * BS, (k + 1) * BS)
                these = [products[i, at, lanes] for i in range(BATCH)]
                for row in range(ROWS):
                    gained = masks[row][0] * these[0]
                    for i in range(1, BATCH):
                        gained += masks[row][i] * these[i]
                    total[row, at, lanes] = total[row, at, lanes] + gained
            return inner

        lax.fori_loop(0, WIDE // 8, add, 0)
        return carry

    total[...] = jnp.zeros_like(total)
    lax.fori_loop(0, RING // BATCH, batch, 0)

    def measure(row, carry):
        for way, k in ((0, 0), (1, 2)):
            top = jnp.zeros((8, WIDE), jnp.float32)
            for chunk in range(k * BS, (k + 1) * BS, 8):
                top = jnp.maximum(top, jnp.abs(total[row, chunk : chunk + 8, :]))
            steps[way, pl.ds(row, 1), :] = jnp.max(top, axis=0, keepdims=True) * (1.0 / LEVELS)
        return carry

    lax.fori_loop(0, ROWS, measure, 0)
    ways = ((0, 0, before), (1, 2, ahead))
    slab_copies = []
    for way, k, peer in ways:
        copy = pltpu.make_async_remote_copy(
            src_ref=steps.at[way],
            dst_ref=steps_in.at[way],
            send_sem=step_send.at[way],
            recv_sem=step_recv.at[way],
            device_id=on_col(peer),
            device_id_type=MESH,
        )
        copy.start()
        slab_copies.append(copy)

    def encode(row, carry):
        for way, k, peer in ways:
            step = steps[way, pl.ds(row, 1), :]
            inverse = jnp.where(step > 0.0, 1.0 / step, 0.0)
            scaled = total[row, k * BS : (k + 1) * BS, :] * inverse
            scaled = jnp.clip(jnp.round(scaled), -LEVELS, LEVELS)
            codes[way, row] = scaled.astype(jnp.int32).astype(jnp.int16)
            pltpu.make_async_remote_copy(
                src_ref=codes.at[way, row],
                dst_ref=codes_in.at[way, row],
                send_sem=code_send.at[way, row],
                recv_sem=code_recv.at[way, row],
                device_id=on_col(peer),
                device_id_type=MESH,
            ).start()
        return carry

    lax.fori_loop(0, ROWS, encode, 0)

    for copy in halo_copies:
        copy.wait()
    apply_normal(0)
    part_copies = send_part(0)
    inner0 = sum(halo[0, way] * part[0, k] for way, k in ((1, 0), (0, 1), (2, 2)))
    inner0 += REGULAR * smooth0 * smooth0
    for copy in part_copies:
        copy.wait()
    mapped0 = part[0, 1] + part_in[0, 0] + part_in[0, 1] + REGULAR * smooth0
    smooth_mapped = apply_precond(mapped0)
    halo_copies = send_halo(1, smooth_mapped)
    rho0, curve0 = all_sum(0, [rhs * smooth0, inner0])
    step0 = rho0 / curve0
    for copy in halo_copies:
        copy.wait()
    apply_normal(1)
    part_copies = send_part(1)
    residual1 = rhs - step0 * mapped0
    smooth1 = smooth0 - step0 * smooth_mapped
    inner1 = REGULAR * smooth1 * smooth1
    cross1 = REGULAR * smooth1 * smooth0
    for way, k in ((1, 0), (0, 1), (2, 2)):
        here = halo[0, way] - step0 * halo[1, way]
        inner1 += here * (part[0, k] - step0 * part[1, k])
        cross1 += here * part[0, k]
    rho1, curve11, curve10 = all_sum(1, [residual1 * smooth1, inner1, cross1])
    ratio = rho1 / rho0
    step1 = rho1 / (curve11 + 2.0 * ratio * curve10 + ratio * ratio * curve0)
    for copy in part_copies:
        copy.wait()
    mapped_smooth = part[1, 1] + part_in[1, 0] + part_in[1, 1] + REGULAR * smooth_mapped
    mapped1 = (mapped0 - step0 * mapped_smooth) + ratio * mapped0
    solution_ref[...] = step0 * smooth0 + step1 * (smooth1 + ratio * smooth0)
    residual_ref[...] = residual1 - step1 * mapped1

    for copy in slab_copies:
        copy.wait()
    rows_in = lax.broadcasted_iota(jnp.int32, (BS, BS), 0)
    columns_in = lax.broadcasted_iota(jnp.int32, (BS, BS), 1)
    diagonal = jnp.where(rows_in == columns_in, REGULAR, 0.0)

    def finish(row, carry):
        for way, k, peer in ways:
            pltpu.make_async_remote_copy(
                src_ref=codes.at[way, row],
                dst_ref=codes_in.at[way, row],
                send_sem=code_send.at[way, row],
                recv_sem=code_recv.at[way, row],
                device_id=on_col(peer),
                device_id_type=MESH,
            ).wait()

        steps_here = [steps_in[way, pl.ds(row, 1), :] for way in range(2)]

        def block(way, l):
            lanes = slice(l * BS, (l + 1) * BS)
            levels = codes_in[way, row, :, lanes].astype(jnp.int32).astype(jnp.float32)
            return levels * steps_here[way][:, lanes]

        own = slice(BS, 2 * BS)
        normal[row, 0] = total[row, own, BS : 2 * BS] + diagonal + block(0, 0) + block(1, 2)
        normal[row, 1] = block(0, 1)
        normal[row, 2] = total[row, own, 0:BS]
        normal[row, 3] = total[row, own, 2 * BS :]
        normal[row, 4] = block(1, 1)
        normal[row, 5] = block(0, 2)
        normal[row, 6] = block(1, 0)
        pltpu.make_async_copy(normal.at[row], normal_hbm.at[row], out_sem.at[row]).start()
        return carry

    lax.fori_loop(0, ROWS, finish, 0)
    for row in range(ROWS):
        pltpu.make_async_copy(normal.at[row], normal_hbm.at[row], out_sem.at[row]).wait()
    for copy in sends:
        copy.wait_send()


def on_device(coeff, scaling, block_rows, precond, rhs):
    f32, bf16 = jnp.float32, jnp.bfloat16
    vmem = pl.BlockSpec(memory_space=pltpu.VMEM)
    anywhere = pl.BlockSpec(memory_space=pl.ANY)
    dma = pltpu.SemaphoreType.DMA
    return pl.pallas_call(
        kernel,
        out_shape=(
            jax.ShapeDtypeStruct((ROWS, 7, BS, BS), f32),
            jax.ShapeDtypeStruct((ROWS, BS), f32),
            jax.ShapeDtypeStruct((ROWS, BS), f32),
        ),
        in_specs=[anywhere, vmem, pl.BlockSpec(memory_space=pltpu.SMEM), anywhere, vmem],
        out_specs=(anywhere, vmem, vmem),
        scratch_shapes=[
            pltpu.VMEM((RING, 3, BS, BS), bf16),
            pltpu.VMEM((RING, BS), f32),
            pltpu.SMEM((RING,), jnp.int32),
            pltpu.VMEM((RING, 3, BS, BS), bf16),
            pltpu.VMEM((RING, 2, BS), f32),
            pltpu.VMEM((RING, 3, BS, BS), bf16),
            pltpu.VMEM((RING, 2, BS), f32),
            pltpu.VMEM((BATCH, WIDE, WIDE), f32),
            pltpu.VMEM((ROWS, WIDE, WIDE), f32),
            pltpu.VMEM((ROWS, BS, BS), f32),
            pltpu.VMEM((ROWS, WIDE, BS), f32),
            pltpu.VMEM((ROWS, BS, BS), f32),
            pltpu.VMEM((2, 3, ROWS, BS), f32),
            pltpu.VMEM((2, 3, ROWS, BS), f32),
            pltpu.VMEM((2, 2, ROWS, BS), f32),
            pltpu.VMEM((2, ROWS, BS, WIDE), jnp.int16),
            pltpu.VMEM((2, ROWS, BS, WIDE), jnp.int16),
            pltpu.VMEM((2, ROWS, WIDE), f32),
            pltpu.VMEM((2, ROWS, WIDE), f32),
            pltpu.VMEM((ROWS, 7, BS, BS), f32),
            pltpu.VMEM((2, 8, 8, BS), f32),
            pltpu.VMEM((2, 4, 8, BS), f32),
            pltpu.VMEM((2, 8, 8, BS), f32),
            dma((2,)),
            dma((RING,)),
            dma((RING,)),
            dma((RING,)),
            dma((RING,)),
            dma((2, 3)),
            dma((2, 3)),
            dma((2, 2)),
            dma((2, 2)),
            dma((2, ROWS)),
            dma((2, ROWS)),
            dma((2,)),
            dma((2,)),
            dma((2, 20)),
            dma((2, 20)),
            dma((ROWS,)),
        ],
        compiler_params=pltpu.CompilerParams(
            collective_id=0, has_side_effects=True, vmem_limit_bytes=56 << 20
        ),
    )(coeff, scaling, block_rows, precond, rhs)


def solution(mesh):
    whole = P(("grp", "col"))
    return jax.shard_map(
        on_device,
        mesh=mesh,
        in_specs=(whole,) * 5,
        out_specs=(whole,) * 3,
        check_vma=False,
    )
```

```python
import jax
import jax.numpy as jnp
from jax import lax
from jax.experimental import pallas as pl
from jax.experimental.pallas import tpu as pltpu
from jax.sharding import PartitionSpec as P

MESH = pl.DeviceIdType.MESH
RING = 32
ROWS = 8
BS = 128
WIDE = 3 * BS
LAYERS = 8
BATCH = 4
REGULAR = 0.5
LEVELS = 32767.0

_GROUPS = (
    ((1, 0), (3, 0), (0, 1), (0, 3)),
    ((2, 0), (0, 2)),
    ((1, 1), (3, 3)),
    ((1, 3), (3, 1)),
    ((2, 1), (2, 3), (1, 2), (3, 2)),
    ((2, 2),),
)
MOVES = [(0, 0, 0), (0, 0, 1)] + [
    (dx, dy, dc) for group in _GROUPS for dc in (0, 1) for dx, dy in group
]


def moved(me, move):
    dx, dy, dc = move
    return (
        lax.rem(me // 8 + dx, 4) * 8
        + lax.rem(lax.rem(me // 2, 4) + dy, 4) * 2
        + lax.rem(me + dc, 2)
    )


def on_col(index):
    return {"col": index}


def spread(columns, first, out, lead):
    out[lead] = jnp.broadcast_to(columns[:, first : first + 1], (BS, BS))


def kernel(
    coeff_hbm,
    scaling_ref,
    rows_ref,
    precond_hbm,
    rhs_ref,
    codes_in,
    steps_in,
    own_hbm,
    solution_ref,
    residual_ref,
    coeff,
    scale32,
    pick,
    stage,
    stage_meta,
    arrived,
    arrived_meta,
    products,
    total,
    precond,
    wide,
    wide_own,
    halo,
    part,
    part_in,
    codes,
    steps,
    steps_land,
    red_z,
    red_p,
    load_sem,
    send_sem,
    recv_sem,
    meta_send,
    meta_recv,
    halo_send,
    halo_recv,
    part_send,
    part_recv,
    code_send,
    code_recv,
    step_send,
    step_recv,
    red_send,
    red_recv,
    out_sem,
):
    me = lax.axis_index("col")
    layer = lax.axis_index("grp")
    before, after = lax.rem(me + RING - 1, RING), lax.rem(me + 1, RING)
    ahead, behind = lax.rem(me + 2, RING), lax.rem(me + RING - 2, RING)
    peers = [moved(me, move) for move in MOVES]

    load = pltpu.make_async_copy(coeff_hbm, coeff, load_sem.at[0])
    load.start()
    load_precond = pltpu.make_async_copy(precond_hbm, precond, load_sem.at[1])
    load_precond.start()

    barrier = pltpu.get_barrier_semaphore()
    for peer in peers[1:]:
        pl.semaphore_signal(barrier, inc=1, device_id=on_col(peer), device_id_type=MESH)
    for other in range(1, LAYERS):
        pl.semaphore_signal(
            barrier, inc=1, device_id={"grp": layer ^ other}, device_id_type=MESH
        )

    scale32[...] = scaling_ref[...].astype(jnp.float32)
    first_row = layer * (RING * ROWS)
    for slot in range(RING):
        home = lax.rem(peers[slot] + RING - 1, RING) * ROWS + first_row
        found = jnp.int32(0)
        for j in range(RING):
            local = rows_ref[0, j] - home
            found = jnp.where((local >= 0) & (local < ROWS), j * ROWS + local, found)
        pick[slot] = found

    def transposed(pieces):
        rows = [*pieces, jnp.zeros((BS - ROWS * len(pieces), BS), jnp.float32)]
        return jnp.transpose(jnp.concatenate(rows, axis=0))

    def apply_precond(vector):
        columns = transposed([vector])
        for row in range(ROWS):
            spread(columns, row, wide_own, row)
        outs = []
        for row in range(ROWS):
            acc = jnp.zeros((8, BS), jnp.float32)
            for chunk in range(0, BS, 8):
                acc += precond[row, chunk : chunk + 8, :] * wide_own[row, chunk : chunk + 8, :]
            outs.append(jnp.sum(acc, axis=0, keepdims=True))
        return jnp.concatenate(outs, axis=0)

    def send_halo(turn, vector):
        halo[turn, 0] = vector
        copies = []
        for way, peer in ((1, after), (2, behind)):
            copy = pltpu.make_async_remote_copy(
                src_ref=halo.at[turn, 0],
                dst_ref=halo.at[turn, way],
                send_sem=halo_send.at[turn, way],
                recv_sem=halo_recv.at[turn, way],
                device_id=on_col(peer),
                device_id_type=MESH,
            )
            copy.start()
            copies.append(copy)
        return copies

    def widen(turn):
        columns = transposed([halo[turn, 1], halo[turn, 0], halo[turn, 2]])
        for row in range(ROWS):
            for k in range(3):
                wide[row, k * BS : (k + 1) * BS, :] = jnp.broadcast_to(
                    columns[:, k * ROWS + row : k * ROWS + row + 1], (BS, BS)
                )

    def apply_normal(turn):
        def one(row, carry):
            acc = [jnp.zeros((8, BS), jnp.float32) for _ in range(3)]
            for chunk in range(0, WIDE, 8):
                v = wide[row, chunk : chunk + 8, :]
                for k in range(3):
                    acc[k] += total[row, chunk : chunk + 8, k * BS : (k + 1) * BS] * v
            for k in range(3):
                part[turn, k, pl.ds(row, 1), :] = jnp.sum(acc[k], axis=0, keepdims=True)
            return carry

        lax.fori_loop(0, ROWS, one, 0)

    def send_part(turn):
        copies = []
        for k, way, peer in ((0, 0, before), (2, 1, ahead)):
            copy = pltpu.make_async_remote_copy(
                src_ref=part.at[turn, k],
                dst_ref=part_in.at[turn, way],
                send_sem=part_send.at[turn, way],
                recv_sem=part_recv.at[turn, way],
                device_id=on_col(peer),
                device_id_type=MESH,
            )
            copy.start()
            copies.append(copy)
        return copies

    def gather(buffer, turn, base, count, target, value):
        buffer[turn, 0] = value
        copies = []
        for t in range(1, count):
            copy = pltpu.make_async_remote_copy(
                src_ref=buffer.at[turn, 0],
                dst_ref=buffer.at[turn, t],
                send_sem=red_send.at[turn, base + t],
                recv_sem=red_recv.at[turn, base + t],
                device_id=target(t),
                device_id_type=MESH,
            )
            copy.start()
            copies.append(copy)
        return copies

    def sum_start(turn, values):
        rows = [jnp.sum(v, axis=0, keepdims=True) for v in values]
        rows.append(jnp.zeros((8 - len(rows), BS), jnp.float32))
        value = jnp.concatenate(rows, axis=0)
        return gather(red_z, turn, 0, LAYERS, lambda t: {"grp": layer ^ t}, value)

    def sum_middle(turn, copies):
        for copy in copies:
            copy.wait()
        value = jnp.sum(red_z[turn], axis=0)
        return gather(red_p, turn, LAYERS, RING, lambda t: {"col": me ^ t}, value)

    def sum_end(turn, copies):
        for copy in copies:
            copy.wait()
        sums = jnp.sum(jnp.sum(red_p[turn], axis=0), axis=1, keepdims=True)
        return [sums[i : i + 1, :] for i in range(3)]

    load.wait()

    def place(slot, blocks, meta):
        found = pick[slot]
        source = found // ROWS
        blocks[slot] = coeff[source]
        meta[slot, 0:1] = scale32[pl.ds(source, 1), :]
        meta[slot, 1:2] = jnp.full((1, BS), lax.rem(found, ROWS), jnp.int32).astype(jnp.float32)

    place(0, arrived, arrived_meta)
    for slot in range(1, RING):
        place(slot, stage, stage_meta)
    load_precond.wait()
    rhs = rhs_ref[...]
    smooth0 = apply_precond(rhs)

    pl.semaphore_wait(barrier, RING - 1 + LAYERS - 1)
    halo_copies = send_halo(0, smooth0)
    sends = []
    for slot in range(1, RING):
        for source, target, out, into in (
            (stage_meta, arrived_meta, meta_send, meta_recv),
            (stage, arrived, send_sem, recv_sem),
        ):
            copy = pltpu.make_async_remote_copy(
                src_ref=source.at[slot],
                dst_ref=target.at[slot],
                send_sem=out.at[slot],
                recv_sem=into.at[slot],
                device_id=on_col(peers[slot]),
                device_id_type=MESH,
            )
            copy.start()
            sends.append(copy)

    def batch(number, carry):
        for i in range(BATCH):
            slot = number * BATCH + i

            @pl.when(slot > 0)
            def _():
                for source, target, out, into in (
                    (stage_meta, arrived_meta, meta_send, meta_recv),
                    (stage, arrived, send_sem, recv_sem),
                ):
                    pltpu.make_async_remote_copy(
                        src_ref=source.at[slot],
                        dst_ref=target.at[slot],
                        send_sem=out.at[slot],
                        recv_sem=into.at[slot],
                        device_id=on_col(after),
                        device_id_type=MESH,
                    ).wait_recv()

            blocks = arrived[slot].reshape(WIDE, BS)
            scaled = blocks.astype(jnp.float32) * arrived_meta[slot, 0:1]
            high = scaled.astype(jnp.bfloat16)
            low = (scaled - high.astype(jnp.float32)).astype(jnp.bfloat16)
            products[i] = lax.dot_general(
                jnp.concatenate([high, low], axis=1),
                jnp.concatenate([blocks, blocks], axis=1),
                (((1,), (1,)), ((), ())),
                preferred_element_type=jnp.float32,
            )
        rows_at = [
            jnp.broadcast_to(arrived_meta[number * BATCH + i, 1:2], (8, BS)) for i in range(BATCH)
        ]
        masks = [
            [jnp.where(at == float(row), 1.0, 0.0) for at in rows_at] for row in range(ROWS)
        ]

        def add(chunk, inner):
            at = pl.ds(pl.multiple_of(chunk * 8, 8), 8)
            for k in range(3):
                lanes = slice(k * BS, (k + 1) * BS)
                these = [products[i, at, lanes] for i in range(BATCH)]
                for row in range(ROWS):
                    gained = masks[row][0] * these[0]
                    for i in range(1, BATCH):
                        gained += masks[row][i] * these[i]
                    total[row, at, lanes] = total[row, at, lanes] + gained
            return inner

        lax.fori_loop(0, WIDE // 8, add, 0)
        return carry

    total[...] = jnp.zeros_like(total)
    lax.fori_loop(0, RING // BATCH // 2, batch, 0)
    for copy in halo_copies:
        copy.wait()
    widen(0)
    lax.fori_loop(RING // BATCH // 2, RING // BATCH, batch, 0)

    own_copies = [
        pltpu.make_async_copy(total.at[row, BS : 2 * BS], own_hbm.at[row], out_sem.at[row])
        for row in range(ROWS)
    ]
    for copy in own_copies:
        copy.start()
    slab_copies = []

    def encode(row):
        for way, k, peer in ((1, 2, ahead), (0, 0, before)):
            slab = total[row, k * BS : (k + 1) * BS, :]
            step = jnp.max(jnp.abs(slab), axis=0, keepdims=True) * (1.0 / LEVELS)
            steps[way, row : row + 1, :] = step
            inverse = jnp.where(step > 0.0, 1.0 / step, 0.0)
            scaled = jnp.clip(jnp.round(slab * inverse), -LEVELS, LEVELS)
            codes[way, row] = scaled.astype(jnp.int32).astype(jnp.int16)
            copy = pltpu.make_async_remote_copy(
                src_ref=codes.at[way, row],
                dst_ref=codes_in.at[way, row],
                send_sem=code_send.at[way, row],
                recv_sem=code_recv.at[way, row],
                device_id=on_col(peer),
                device_id_type=MESH,
            )
            copy.start()
            slab_copies.append(copy)

    apply_normal(0)
    part_copies = send_part(0)
    inner0 = sum(halo[0, way] * part[0, k] for way, k in ((1, 0), (0, 1), (2, 2)))
    inner0 += REGULAR * smooth0 * smooth0
    sum_copies = sum_start(0, [rhs * smooth0, inner0])
    encode(0)
    encode(1)
    for copy in part_copies:
        copy.wait()
    mapped0 = part[0, 1] + part_in[0, 0] + part_in[0, 1] + REGULAR * smooth0
    smooth_mapped = apply_precond(mapped0)
    halo_copies = send_halo(1, smooth_mapped)
    sum_copies = sum_middle(0, sum_copies)
    encode(2)
    encode(3)
    for copy in halo_copies:
        copy.wait()
    widen(1)
    apply_normal(1)
    part_copies = send_part(1)
    rho0, curve0, _ = sum_end(0, sum_copies)
    step0 = rho0 / curve0
    residual1 = rhs - step0 * mapped0
    smooth1 = smooth0 - step0 * smooth_mapped
    inner1 = REGULAR * smooth1 * smooth1
    cross1 = REGULAR * smooth1 * smooth0
    for way, k in ((1, 0), (0, 1), (2, 2)):
        here = halo[0, way] - step0 * halo[1, way]
        inner1 += here * (part[0, k] - step0 * part[1, k])
        cross1 += here * part[0, k]
    sum_copies = sum_start(1, [residual1 * smooth1, inner1, cross1])
    encode(4)
    encode(5)
    sum_copies = sum_middle(1, sum_copies)
    encode(6)
    encode(7)
    for way, peer in ((1, ahead), (0, before)):
        copy = pltpu.make_async_remote_copy(
            src_ref=steps.at[way],
            dst_ref=steps_land.at[way],
            send_sem=step_send.at[way],
            recv_sem=step_recv.at[way],
            device_id=on_col(peer),
            device_id_type=MESH,
        )
        copy.start()
        slab_copies.append(copy)
    for copy in part_copies:
        copy.wait()
    mapped_smooth = part[1, 1] + part_in[1, 0] + part_in[1, 1] + REGULAR * smooth_mapped
    rho1, curve11, curve10 = sum_end(1, sum_copies)
    ratio = rho1 / rho0
    step1 = rho1 / (curve11 + 2.0 * ratio * curve10 + ratio * ratio * curve0)
    mapped1 = (mapped0 - step0 * mapped_smooth) + ratio * mapped0
    solution_ref[...] = step0 * smooth0 + step1 * (smooth1 + ratio * smooth0)
    residual_ref[...] = residual1 - step1 * mapped1

    for copy in slab_copies:
        copy.wait()
    steps_in[...] = steps_land[...]
    for copy in own_copies:
        copy.wait()
    for copy in sends:
        copy.wait_send()


def finish(codes_ref, steps_ref, own_ref, solution_ref, residual_ref, normal_ref, x_ref, r_ref):
    rows_in = lax.broadcasted_iota(jnp.int32, (BS, BS), 0)
    columns_in = lax.broadcasted_iota(jnp.int32, (BS, BS), 1)
    diagonal = jnp.where(rows_in == columns_in, REGULAR, 0.0)
    x_ref[...] = solution_ref[...]
    r_ref[...] = residual_ref[...]
    steps = [steps_ref[way, pl.ds(pl.program_id(0), 1), :] for way in range(2)]

    def block(way, l):
        lanes = slice(l * BS, (l + 1) * BS)
        return codes_ref[way, 0, :, lanes].astype(jnp.int32).astype(jnp.float32) * steps[way][:, lanes]

    normal_ref[0, 0] = own_ref[0, :, BS : 2 * BS] + diagonal + block(0, 0) + block(1, 2)
    normal_ref[0, 1] = block(0, 1)
    normal_ref[0, 2] = own_ref[0, :, 0:BS]
    normal_ref[0, 3] = own_ref[0, :, 2 * BS :]
    normal_ref[0, 4] = block(1, 1)
    normal_ref[0, 5] = block(0, 2)
    normal_ref[0, 6] = block(1, 0)


def on_device(coeff, scaling, block_rows, precond, rhs):
    f32, bf16 = jnp.float32, jnp.bfloat16
    vmem = pl.BlockSpec(memory_space=pltpu.VMEM)
    anywhere = pl.BlockSpec(memory_space=pl.ANY)
    dma = pltpu.SemaphoreType.DMA
    codes, steps, own, x, r = pl.pallas_call(
        kernel,
        out_shape=(
            jax.ShapeDtypeStruct((2, ROWS, BS, WIDE), jnp.int16),
            jax.ShapeDtypeStruct((2, ROWS, WIDE), f32),
            jax.ShapeDtypeStruct((ROWS, BS, WIDE), f32),
            jax.ShapeDtypeStruct((ROWS, BS), f32),
            jax.ShapeDtypeStruct((ROWS, BS), f32),
        ),
        in_specs=[anywhere, vmem, pl.BlockSpec(memory_space=pltpu.SMEM), anywhere, vmem],
        out_specs=(anywhere, vmem, anywhere, vmem, vmem),
        scratch_shapes=[
            pltpu.VMEM((RING, 3, BS, BS), bf16),
            pltpu.VMEM((RING, BS), f32),
            pltpu.SMEM((RING,), jnp.int32),
            pltpu.VMEM((RING, 3, BS, BS), bf16),
            pltpu.VMEM((RING, 2, BS), f32),
            pltpu.VMEM((RING, 3, BS, BS), bf16),
            pltpu.VMEM((RING, 2, BS), f32),
            pltpu.VMEM((BATCH, WIDE, WIDE), f32),
            pltpu.VMEM((ROWS, WIDE, WIDE), f32),
            pltpu.VMEM((ROWS, BS, BS), f32),
            pltpu.VMEM((ROWS, WIDE, BS), f32),
            pltpu.VMEM((ROWS, BS, BS), f32),
            pltpu.VMEM((2, 3, ROWS, BS), f32),
            pltpu.VMEM((2, 3, ROWS, BS), f32),
            pltpu.VMEM((2, 2, ROWS, BS), f32),
            pltpu.VMEM((2, ROWS, BS, WIDE), jnp.int16),
            pltpu.VMEM((2, ROWS, WIDE), f32),
            pltpu.VMEM((2, ROWS, WIDE), f32),
            pltpu.VMEM((2, LAYERS, 8, BS), f32),
            pltpu.VMEM((2, RING, 8, BS), f32),
            dma((2,)),
            dma((RING,)),
            dma((RING,)),
            dma((RING,)),
            dma((RING,)),
            dma((2, 3)),
            dma((2, 3)),
            dma((2, 2)),
            dma((2, 2)),
            dma((2, ROWS)),
            dma((2, ROWS)),
            dma((2,)),
            dma((2,)),
            dma((2, LAYERS + RING)),
            dma((2, LAYERS + RING)),
            dma((ROWS,)),
        ],
        compiler_params=pltpu.CompilerParams(
            collective_id=0, has_side_effects=True, vmem_limit_bytes=56 << 20
        ),
    )(coeff, scaling, block_rows.T, precond, rhs)
    small = pl.BlockSpec((ROWS, BS), lambda row: (0, 0))
    return pl.pallas_call(
        finish,
        grid=(ROWS,),
        out_shape=(
            jax.ShapeDtypeStruct((ROWS, 7, BS, BS), f32),
            jax.ShapeDtypeStruct((ROWS, BS), f32),
            jax.ShapeDtypeStruct((ROWS, BS), f32),
        ),
        in_specs=[
            pl.BlockSpec((2, 1, BS, WIDE), lambda row: (0, row, 0, 0)),
            pl.BlockSpec((2, ROWS, WIDE), lambda row: (0, 0, 0)),
            pl.BlockSpec((1, BS, WIDE), lambda row: (row, 0, 0)),
            small,
            small,
        ],
        out_specs=(pl.BlockSpec((1, 7, BS, BS), lambda row: (row, 0, 0, 0)), small, small),
    )(codes, steps, own, x, r)


def solution(mesh):
    whole = P(("grp", "col"))
    return jax.shard_map(
        on_device,
        mesh=mesh,
        in_specs=(whole,) * 5,
        out_specs=(whole,) * 3,
        check_vma=False,
    )
```

```python
import jax
import jax.numpy as jnp
from jax import lax
from jax.experimental import pallas as pl
from jax.experimental.pallas import tpu as pltpu
from jax.sharding import PartitionSpec as P

MESH = pl.DeviceIdType.MESH
RING = 32
ROWS = 8
BS = 128
WIDE = 3 * BS
LAYERS = 8
BATCH = 4
EARLY = 9
REGULAR = 0.5
LEVELS = 32767.0

_GROUPS = (
    ((1, 0), (3, 0), (0, 1), (0, 3)),
    ((2, 0), (0, 2)),
    ((1, 1), (3, 3)),
    ((1, 3), (3, 1)),
    ((2, 1), (2, 3), (1, 2), (3, 2)),
    ((2, 2),),
)
MOVES = [(0, 0, 0), (0, 0, 1)] + [
    (dx, dy, dc) for group in _GROUPS for dc in (0, 1) for dx, dy in group
]


def moved(me, move):
    dx, dy, dc = move
    return (
        lax.rem(me // 8 + dx, 4) * 8
        + lax.rem(lax.rem(me // 2, 4) + dy, 4) * 2
        + lax.rem(me + dc, 2)
    )


def on_col(index):
    return {"col": index}


def spread(columns, first, out, lead):
    out[lead] = jnp.broadcast_to(columns[:, first : first + 1], (BS, BS))


def kernel(
    coeff_hbm,
    scaling_ref,
    rows_ref,
    precond_hbm,
    rhs_ref,
    codes_in,
    steps_in,
    own_hbm,
    solution_ref,
    residual_ref,
    coeff,
    scale32,
    stage,
    stage_meta,
    arrived,
    arrived_meta,
    products,
    total,
    precond,
    wide,
    wide_own,
    halo,
    part,
    part_in,
    codes,
    steps,
    steps_land,
    red_z,
    red_p,
    load_sem,
    send_sem,
    recv_sem,
    meta_send,
    meta_recv,
    halo_send,
    halo_recv,
    part_send,
    part_recv,
    code_send,
    code_recv,
    step_send,
    step_recv,
    red_send,
    red_recv,
    out_sem,
):
    me = lax.axis_index("col")
    layer = lax.axis_index("grp")
    before, after = lax.rem(me + RING - 1, RING), lax.rem(me + 1, RING)
    ahead, behind = lax.rem(me + 2, RING), lax.rem(me + RING - 2, RING)
    peers = [moved(me, move) for move in MOVES]

    load = pltpu.make_async_copy(coeff_hbm, coeff, load_sem.at[0])
    load.start()
    load_precond = pltpu.make_async_copy(precond_hbm, precond, load_sem.at[1])
    load_precond.start()

    barrier = pltpu.get_barrier_semaphore()
    for peer in peers[1:]:
        pl.semaphore_signal(barrier, inc=1, device_id=on_col(peer), device_id_type=MESH)
    for other in range(1, LAYERS):
        pl.semaphore_signal(
            barrier, inc=1, device_id={"grp": layer ^ other}, device_id_type=MESH
        )

    scale32[...] = scaling_ref[...].astype(jnp.float32)
    first_row = layer * (RING * ROWS)

    def transposed(pieces):
        rows = [*pieces, jnp.zeros((BS - ROWS * len(pieces), BS), jnp.float32)]
        return jnp.transpose(jnp.concatenate(rows, axis=0))

    def apply_precond(vector):
        columns = transposed([vector])
        for row in range(ROWS):
            spread(columns, row, wide_own, row)
        outs = []
        for row in range(ROWS):
            acc = jnp.zeros((8, BS), jnp.float32)
            for chunk in range(0, BS, 8):
                acc += precond[row, chunk : chunk + 8, :] * wide_own[row, chunk : chunk + 8, :]
            outs.append(jnp.sum(acc, axis=0, keepdims=True))
        return jnp.concatenate(outs, axis=0)

    def send_halo(turn, vector):
        halo[turn, 0] = vector
        copies = []
        for way, peer in ((1, after), (2, behind)):
            copy = pltpu.make_async_remote_copy(
                src_ref=halo.at[turn, 0],
                dst_ref=halo.at[turn, way],
                send_sem=halo_send.at[turn, way],
                recv_sem=halo_recv.at[turn, way],
                device_id=on_col(peer),
                device_id_type=MESH,
            )
            copy.start()
            copies.append(copy)
        return copies

    def widen(turn):
        columns = transposed([halo[turn, 1], halo[turn, 0], halo[turn, 2]])
        for row in range(ROWS):
            for k in range(3):
                wide[row, k * BS : (k + 1) * BS, :] = jnp.broadcast_to(
                    columns[:, k * ROWS + row : k * ROWS + row + 1], (BS, BS)
                )

    def apply_normal(turn):
        def one(row, carry):
            acc = [jnp.zeros((8, BS), jnp.float32) for _ in range(3)]
            for chunk in range(0, WIDE, 8):
                v = wide[row, chunk : chunk + 8, :]
                for k in range(3):
                    acc[k] += total[row, chunk : chunk + 8, k * BS : (k + 1) * BS] * v
            for k in range(3):
                part[turn, k, pl.ds(row, 1), :] = jnp.sum(acc[k], axis=0, keepdims=True)
            return carry

        lax.fori_loop(0, ROWS, one, 0)

    def send_part(turn):
        copies = []
        for k, way, peer in ((0, 0, before), (2, 1, ahead)):
            copy = pltpu.make_async_remote_copy(
                src_ref=part.at[turn, k],
                dst_ref=part_in.at[turn, way],
                send_sem=part_send.at[turn, way],
                recv_sem=part_recv.at[turn, way],
                device_id=on_col(peer),
                device_id_type=MESH,
            )
            copy.start()
            copies.append(copy)
        return copies

    def gather(buffer, turn, base, count, target, value):
        buffer[turn, 0] = value
        copies = []
        for t in range(1, count):
            copy = pltpu.make_async_remote_copy(
                src_ref=buffer.at[turn, 0],
                dst_ref=buffer.at[turn, t],
                send_sem=red_send.at[turn, base + t],
                recv_sem=red_recv.at[turn, base + t],
                device_id=target(t),
                device_id_type=MESH,
            )
            copy.start()
            copies.append(copy)
        return copies

    def sum_start(turn, values):
        lane = lax.broadcasted_iota(jnp.int32, (1, BS), 1)
        value = jnp.zeros((1, BS), jnp.float32)
        for i, v in enumerate(values):
            value = jnp.where(lane == i, jnp.sum(v, keepdims=True), value)
        return gather(red_z, turn, 0, LAYERS, lambda t: {"grp": layer ^ t}, value)

    def sum_middle(turn, copies):
        for copy in copies:
            copy.wait()
        value = jnp.sum(red_z[turn], axis=0)
        return gather(red_p, turn, LAYERS, RING, lambda t: {"col": me ^ t}, value)

    def sum_end(turn, copies):
        for copy in copies:
            copy.wait()
        sums = jnp.sum(red_p[turn], axis=0)
        lane = lax.broadcasted_iota(jnp.int32, (1, BS), 1)
        return [jnp.sum(jnp.where(lane == i, sums, 0.0), keepdims=True) for i in range(3)]

    def place(slot, blocks, meta):
        home = lax.rem(peers[slot] + RING - 1, RING) * ROWS + first_row
        found = jnp.int32(0)
        for j in range(RING):
            local = rows_ref[0, j] - home
            found = jnp.where((local >= 0) & (local < ROWS), j * ROWS + local, found)
        source = found // ROWS
        blocks[slot] = coeff[source]
        meta[slot, 0:1] = scale32[pl.ds(source, 1), :]
        meta[slot, 1:2] = jnp.full((1, BS), lax.rem(found, ROWS), jnp.int32).astype(jnp.float32)

    def send_block(slot):
        place(slot, stage, stage_meta)
        copies = []
        for source, target, out, into in (
            (stage_meta, arrived_meta, meta_send, meta_recv),
            (stage, arrived, send_sem, recv_sem),
        ):
            copy = pltpu.make_async_remote_copy(
                src_ref=source.at[slot],
                dst_ref=target.at[slot],
                send_sem=out.at[slot],
                recv_sem=into.at[slot],
                device_id=on_col(peers[slot]),
                device_id_type=MESH,
            )
            copy.start()
            copies.append(copy)
        return copies

    load.wait()
    place(0, arrived, arrived_meta)
    pl.semaphore_wait(barrier, RING - 1 + LAYERS - 1)
    sends = []
    for slot in range(1, EARLY):
        sends += send_block(slot)
    load_precond.wait()
    rhs = rhs_ref[...]
    smooth0 = apply_precond(rhs)
    halo_copies = send_halo(0, smooth0)
    for slot in range(EARLY, RING):
        sends += send_block(slot)

    def batch(first, count):
        for i in range(count):
            slot = first + i

            @pl.when(slot > 0)
            def _():
                for source, target, out, into in (
                    (stage_meta, arrived_meta, meta_send, meta_recv),
                    (stage, arrived, send_sem, recv_sem),
                ):
                    pltpu.make_async_remote_copy(
                        src_ref=source.at[slot],
                        dst_ref=target.at[slot],
                        send_sem=out.at[slot],
                        recv_sem=into.at[slot],
                        device_id=on_col(after),
                        device_id_type=MESH,
                    ).wait_recv()

            blocks = arrived[slot].reshape(WIDE, BS)
            scaled = blocks.astype(jnp.float32) * arrived_meta[slot, 0:1]
            high = scaled.astype(jnp.bfloat16)
            low = (scaled - high.astype(jnp.float32)).astype(jnp.bfloat16)
            products[i] = lax.dot_general(
                jnp.concatenate([high, low], axis=1),
                jnp.concatenate([blocks, blocks], axis=1),
                (((1,), (1,)), ((), ())),
                preferred_element_type=jnp.float32,
            )
        rows_at = [
            jnp.broadcast_to(arrived_meta[first + i, 1:2], (8, BS)) for i in range(count)
        ]
        masks = [
            [jnp.where(at == float(row), 1.0, 0.0) for at in rows_at] for row in range(ROWS)
        ]

        def add(chunk, inner):
            at = pl.ds(pl.multiple_of(chunk * 8, 8), 8)
            for k in range(3):
                lanes = slice(k * BS, (k + 1) * BS)
                these = [products[i, at, lanes] for i in range(count)]
                for row in range(ROWS):
                    gained = masks[row][0] * these[0]
                    for i in range(1, count):
                        gained += masks[row][i] * these[i]
                    total[row, at, lanes] = total[row, at, lanes] + gained
            return inner

        lax.fori_loop(0, WIDE // 8, add, 0)

    def full_batch(number, carry):
        batch(number * BATCH, BATCH)
        return carry

    total[...] = jnp.zeros_like(total)
    lax.fori_loop(0, RING // BATCH // 2, full_batch, 0)
    for copy in halo_copies:
        copy.wait()
    widen(0)
    lax.fori_loop(RING // BATCH // 2, RING // BATCH - 1, full_batch, 0)
    batch(RING - 4, 2)
    batch(RING - 2, 2)

    own_copies = [
        pltpu.make_async_copy(total.at[row, BS : 2 * BS], own_hbm.at[row], out_sem.at[row])
        for row in range(ROWS)
    ]
    for copy in own_copies:
        copy.start()
    slab_copies = []

    def encode(row):
        for way, k, peer in ((1, 2, ahead), (0, 0, before)):
            slab = total[row, k * BS : (k + 1) * BS, :]
            step = jnp.max(jnp.abs(slab), axis=0, keepdims=True) * (1.0 / LEVELS)
            steps[way, row : row + 1, :] = step
            inverse = jnp.where(step > 0.0, 1.0 / step, 0.0)
            scaled = jnp.clip(jnp.round(slab * inverse), -LEVELS, LEVELS)
            codes[way, row] = scaled.astype(jnp.int32).astype(jnp.int16)
            copy = pltpu.make_async_remote_copy(
                src_ref=codes.at[way, row],
                dst_ref=codes_in.at[way, row],
                send_sem=code_send.at[way, row],
                recv_sem=code_recv.at[way, row],
                device_id=on_col(peer),
                device_id_type=MESH,
            )
            copy.start()
            slab_copies.append(copy)

    apply_normal(0)
    part_copies = send_part(0)
    inner0 = sum(halo[0, way] * part[0, k] for way, k in ((1, 0), (0, 1), (2, 2)))
    inner0 += REGULAR * smooth0 * smooth0
    sum_copies = sum_start(0, [rhs * smooth0, inner0])
    encode(0)
    encode(1)
    for copy in part_copies:
        copy.wait()
    mapped0 = part[0, 1] + part_in[0, 0] + part_in[0, 1] + REGULAR * smooth0
    smooth_mapped = apply_precond(mapped0)
    halo_copies = send_halo(1, smooth_mapped)
    sum_copies = sum_middle(0, sum_copies)
    encode(2)
    encode(3)
    for copy in halo_copies:
        copy.wait()
    widen(1)
    apply_normal(1)
    part_copies = send_part(1)
    rho0, curve0, _ = sum_end(0, sum_copies)
    step0 = rho0 / curve0
    residual1 = rhs - step0 * mapped0
    smooth1 = smooth0 - step0 * smooth_mapped
    inner1 = REGULAR * smooth1 * smooth1
    cross1 = REGULAR * smooth1 * smooth0
    for way, k in ((1, 0), (0, 1), (2, 2)):
        here = halo[0, way] - step0 * halo[1, way]
        inner1 += here * (part[0, k] - step0 * part[1, k])
        cross1 += here * part[0, k]
    sum_copies = sum_start(1, [residual1 * smooth1, inner1, cross1])
    encode(4)
    encode(5)
    sum_copies = sum_middle(1, sum_copies)
    encode(6)
    encode(7)
    for way, peer in ((1, ahead), (0, before)):
        copy = pltpu.make_async_remote_copy(
            src_ref=steps.at[way],
            dst_ref=steps_land.at[way],
            send_sem=step_send.at[way],
            recv_sem=step_recv.at[way],
            device_id=on_col(peer),
            device_id_type=MESH,
        )
        copy.start()
        slab_copies.append(copy)
    for copy in part_copies:
        copy.wait()
    mapped_smooth = part[1, 1] + part_in[1, 0] + part_in[1, 1] + REGULAR * smooth_mapped
    rho1, curve11, curve10 = sum_end(1, sum_copies)
    ratio = rho1 / rho0
    step1 = rho1 / (curve11 + 2.0 * ratio * curve10 + ratio * ratio * curve0)
    mapped1 = (mapped0 - step0 * mapped_smooth) + ratio * mapped0
    solution_ref[...] = step0 * smooth0 + step1 * (smooth1 + ratio * smooth0)
    residual_ref[...] = residual1 - step1 * mapped1

    for copy in slab_copies:
        copy.wait()
    steps_in[...] = steps_land[...]
    for copy in own_copies:
        copy.wait()
    for copy in sends:
        copy.wait_send()


def finish(
    codes_hbm,
    steps_ref,
    own_hbm,
    solution_ref,
    residual_ref,
    normal_hbm,
    x_ref,
    r_ref,
    codes,
    own,
    normal,
    load_sem,
    out_sem,
):
    loads = [
        [
            pltpu.make_async_copy(codes_hbm.at[0, row], codes.at[0, row], load_sem.at[0, row]),
            pltpu.make_async_copy(codes_hbm.at[1, row], codes.at[1, row], load_sem.at[1, row]),
            pltpu.make_async_copy(own_hbm.at[row], own.at[row], load_sem.at[2, row]),
        ]
        for row in range(ROWS)
    ]
    for copies in loads:
        for copy in copies:
            copy.start()
    rows_in = lax.broadcasted_iota(jnp.int32, (BS, BS), 0)
    columns_in = lax.broadcasted_iota(jnp.int32, (BS, BS), 1)
    diagonal = jnp.where(rows_in == columns_in, REGULAR, 0.0)
    x_ref[...] = solution_ref[...]
    r_ref[...] = residual_ref[...]
    outs = []
    for row in range(ROWS):
        for copy in loads[row]:
            copy.wait()

        def block(way, l):
            lanes = slice(l * BS, (l + 1) * BS)
            levels = codes[way, row, :, lanes].astype(jnp.int32).astype(jnp.float32)
            return levels * steps_ref[way, row : row + 1, lanes]

        normal[row, 0] = own[row, :, BS : 2 * BS] + diagonal + block(0, 0) + block(1, 2)
        normal[row, 1] = block(0, 1)
        normal[row, 2] = own[row, :, 0:BS]
        normal[row, 3] = own[row, :, 2 * BS :]
        normal[row, 4] = block(1, 1)
        normal[row, 5] = block(0, 2)
        normal[row, 6] = block(1, 0)
        out = pltpu.make_async_copy(normal.at[row], normal_hbm.at[row], out_sem.at[row])
        out.start()
        outs.append(out)
    for out in outs:
        out.wait()


def on_device(coeff, scaling, block_rows, precond, rhs):
    f32, bf16 = jnp.float32, jnp.bfloat16
    vmem = pl.BlockSpec(memory_space=pltpu.VMEM)
    anywhere = pl.BlockSpec(memory_space=pl.ANY)
    dma = pltpu.SemaphoreType.DMA
    codes, steps, own, x, r = pl.pallas_call(
        kernel,
        out_shape=(
            jax.ShapeDtypeStruct((2, ROWS, BS, WIDE), jnp.int16),
            jax.ShapeDtypeStruct((2, ROWS, WIDE), f32),
            jax.ShapeDtypeStruct((ROWS, BS, WIDE), f32),
            jax.ShapeDtypeStruct((ROWS, BS), f32),
            jax.ShapeDtypeStruct((ROWS, BS), f32),
        ),
        in_specs=[anywhere, vmem, pl.BlockSpec(memory_space=pltpu.SMEM), anywhere, vmem],
        out_specs=(anywhere, vmem, anywhere, vmem, vmem),
        scratch_shapes=[
            pltpu.VMEM((RING, 3, BS, BS), bf16),
            pltpu.VMEM((RING, BS), f32),
            pltpu.VMEM((RING, 3, BS, BS), bf16),
            pltpu.VMEM((RING, 2, BS), f32),
            pltpu.VMEM((RING, 3, BS, BS), bf16),
            pltpu.VMEM((RING, 2, BS), f32),
            pltpu.VMEM((BATCH, WIDE, WIDE), f32),
            pltpu.VMEM((ROWS, WIDE, WIDE), f32),
            pltpu.VMEM((ROWS, BS, BS), f32),
            pltpu.VMEM((ROWS, WIDE, BS), f32),
            pltpu.VMEM((ROWS, BS, BS), f32),
            pltpu.VMEM((2, 3, ROWS, BS), f32),
            pltpu.VMEM((2, 3, ROWS, BS), f32),
            pltpu.VMEM((2, 2, ROWS, BS), f32),
            pltpu.VMEM((2, ROWS, BS, WIDE), jnp.int16),
            pltpu.VMEM((2, ROWS, WIDE), f32),
            pltpu.VMEM((2, ROWS, WIDE), f32),
            pltpu.VMEM((2, LAYERS, 1, BS), f32),
            pltpu.VMEM((2, RING, 1, BS), f32),
            dma((2,)),
            dma((RING,)),
            dma((RING,)),
            dma((RING,)),
            dma((RING,)),
            dma((2, 3)),
            dma((2, 3)),
            dma((2, 2)),
            dma((2, 2)),
            dma((2, ROWS)),
            dma((2, ROWS)),
            dma((2,)),
            dma((2,)),
            dma((2, LAYERS + RING)),
            dma((2, LAYERS + RING)),
            dma((ROWS,)),
        ],
        compiler_params=pltpu.CompilerParams(
            collective_id=0, has_side_effects=True, vmem_limit_bytes=56 << 20
        ),
    )(coeff, scaling, block_rows.T, precond, rhs)
    return pl.pallas_call(
        finish,
        out_shape=(
            jax.ShapeDtypeStruct((ROWS, 7, BS, BS), f32),
            jax.ShapeDtypeStruct((ROWS, BS), f32),
            jax.ShapeDtypeStruct((ROWS, BS), f32),
        ),
        in_specs=[anywhere, vmem, anywhere, vmem, vmem],
        out_specs=(anywhere, vmem, vmem),
        scratch_shapes=[
            pltpu.VMEM((2, ROWS, BS, WIDE), jnp.int16),
            pltpu.VMEM((ROWS, BS, WIDE), f32),
            pltpu.VMEM((ROWS, 7, BS, BS), f32),
            dma((3, ROWS)),
            dma((ROWS,)),
        ],
        compiler_params=pltpu.CompilerParams(vmem_limit_bytes=56 << 20),
    )(codes, steps, own, x, r)


def solution(mesh):
    whole = P(("grp", "col"))
    return jax.shard_map(
        on_device,
        mesh=mesh,
        in_specs=(whole,) * 5,
        out_specs=(whole,) * 3,
        check_vma=False,
    )
```

```python
import jax
import jax.numpy as jnp
from jax import lax
from jax.experimental import pallas as pl
from jax.experimental.pallas import tpu as pltpu
from jax.sharding import PartitionSpec as P

MESH = pl.DeviceIdType.MESH
RING = 32
ROWS = 8
BS = 128
WIDE = 3 * BS
LAYERS = 8
BATCH = 4
EARLY = 9
REGULAR = 0.5
LEVELS = 32767.0

_GROUPS = (
    ((1, 0), (3, 0), (0, 1), (0, 3)),
    ((2, 0), (0, 2)),
    ((1, 1), (3, 3)),
    ((1, 3), (3, 1)),
    ((2, 1), (2, 3), (1, 2), (3, 2)),
    ((2, 2),),
)
MOVES = [(0, 0, 0), (0, 0, 1)] + [
    (dx, dy, dc) for group in _GROUPS for dc in (0, 1) for dx, dy in group
]


def moved(me, move):
    dx, dy, dc = move
    return (
        lax.rem(me // 8 + dx, 4) * 8
        + lax.rem(lax.rem(me // 2, 4) + dy, 4) * 2
        + lax.rem(me + dc, 2)
    )


def on_col(index):
    return {"col": index}


def spread(columns, first, out, lead):
    out[lead] = jnp.broadcast_to(columns[:, first : first + 1], (BS, BS))


def kernel(
    coeff_hbm,
    scaling_hbm,
    rows_hbm,
    precond_hbm,
    rhs_hbm,
    codes_in,
    steps_in,
    own_hbm,
    vectors_hbm,
    coeff,
    rows_ref,
    scaling_ref,
    rhs_ref,
    scale32,
    stage,
    stage_meta,
    arrived,
    arrived_meta,
    products,
    total,
    precond,
    wide,
    wide_own,
    halo,
    part,
    part_in,
    codes,
    steps,
    vectors,
    red_z,
    red_p,
    load_sem,
    send_sem,
    recv_sem,
    meta_send,
    meta_recv,
    halo_send,
    halo_recv,
    part_send,
    part_recv,
    code_send,
    code_recv,
    step_send,
    step_recv,
    red_send,
    red_recv,
    out_sem,
):
    me = lax.axis_index("col")
    layer = lax.axis_index("grp")
    before, after = lax.rem(me + RING - 1, RING), lax.rem(me + 1, RING)
    ahead, behind = lax.rem(me + 2, RING), lax.rem(me + RING - 2, RING)
    peers = [moved(me, move) for move in MOVES]

    load = pltpu.make_async_copy(coeff_hbm, coeff, load_sem.at[0])
    load.start()
    barrier = pltpu.get_barrier_semaphore()
    for other in (4, 3, 5, 2, 6, 1, 7):
        pl.semaphore_signal(
            barrier,
            inc=1,
            device_id={"grp": lax.rem(layer + other, LAYERS)},
            device_id_type=MESH,
        )
    for peer in peers[:0:-1]:
        pl.semaphore_signal(barrier, inc=1, device_id=on_col(peer), device_id_type=MESH)
    small_loads = [
        pltpu.make_async_copy(source, target, load_sem.at[2 + i])
        for i, (source, target) in enumerate(
            ((rows_hbm, rows_ref), (scaling_hbm, scaling_ref), (rhs_hbm, rhs_ref))
        )
    ]
    for copy in small_loads:
        copy.start()
    load_precond = pltpu.make_async_copy(precond_hbm, precond, load_sem.at[1])
    load_precond.start()
    for copy in small_loads:
        copy.wait()

    scale32[...] = scaling_ref[...].astype(jnp.float32)
    first_row = layer * (RING * ROWS)

    def transposed(pieces):
        rows = [*pieces, jnp.zeros((BS - ROWS * len(pieces), BS), jnp.float32)]
        return jnp.transpose(jnp.concatenate(rows, axis=0))

    def apply_precond(vector):
        columns = transposed([vector])
        for row in range(ROWS):
            spread(columns, row, wide_own, row)
        outs = []
        for row in range(ROWS):
            acc = jnp.zeros((8, BS), jnp.float32)
            for chunk in range(0, BS, 8):
                acc += precond[row, chunk : chunk + 8, :] * wide_own[row, chunk : chunk + 8, :]
            outs.append(jnp.sum(acc, axis=0, keepdims=True))
        return jnp.concatenate(outs, axis=0)

    def send_halo(turn, vector):
        halo[turn, 0] = vector
        copies = []
        for way, peer in ((1, after), (2, behind)):
            copy = pltpu.make_async_remote_copy(
                src_ref=halo.at[turn, 0],
                dst_ref=halo.at[turn, way],
                send_sem=halo_send.at[turn, way],
                recv_sem=halo_recv.at[turn, way],
                device_id=on_col(peer),
                device_id_type=MESH,
            )
            copy.start()
            copies.append(copy)
        return copies

    def widen(turn):
        columns = transposed([halo[turn, 1], halo[turn, 0], halo[turn, 2]])
        for row in range(ROWS):
            for k in range(3):
                wide[row, k * BS : (k + 1) * BS, :] = jnp.broadcast_to(
                    columns[:, k * ROWS + row : k * ROWS + row + 1], (BS, BS)
                )

    def apply_normal(turn):
        def one(row, carry):
            acc = [jnp.zeros((8, BS), jnp.float32) for _ in range(3)]
            for chunk in range(0, WIDE, 8):
                v = wide[row, chunk : chunk + 8, :]
                for k in range(3):
                    acc[k] += total[row, chunk : chunk + 8, k * BS : (k + 1) * BS] * v
            for k in range(3):
                part[turn, k, pl.ds(row, 1), :] = jnp.sum(acc[k], axis=0, keepdims=True)
            return carry

        lax.fori_loop(0, ROWS, one, 0)

    def send_part(turn):
        copies = []
        for k, way, peer in ((0, 0, before), (2, 1, ahead)):
            copy = pltpu.make_async_remote_copy(
                src_ref=part.at[turn, k],
                dst_ref=part_in.at[turn, way],
                send_sem=part_send.at[turn, way],
                recv_sem=part_recv.at[turn, way],
                device_id=on_col(peer),
                device_id_type=MESH,
            )
            copy.start()
            copies.append(copy)
        return copies

    lane = lax.broadcasted_iota(jnp.int32, (1, BS), 1)

    def in_lanes(scalars):
        row = jnp.zeros((1, BS), jnp.float32)
        for i, scalar in enumerate(scalars):
            row = jnp.where(lane == i, scalar, row)
        return row

    def out_of_lanes(row, count):
        return [jnp.sum(jnp.where(lane == i, row, 0.0), keepdims=True) for i in range(count)]

    def gather(buffer, turn, base, count, target, value):
        buffer[turn, 0] = value
        copies = []
        for t in range(1, count):
            copy = pltpu.make_async_remote_copy(
                src_ref=buffer.at[turn, 0],
                dst_ref=buffer.at[turn, t],
                send_sem=red_send.at[turn, base + t],
                recv_sem=red_recv.at[turn, base + t],
                device_id=target(t),
                device_id_type=MESH,
            )
            copy.start()
            copies.append(copy)
        return copies

    def plane_start(turn, values):
        row = in_lanes([jnp.sum(v, keepdims=True) for v in values])
        return gather(red_p, turn, LAYERS, RING, lambda t: {"col": me ^ t}, row)

    def layers_start(turn, row):
        return gather(red_z, turn, 0, LAYERS, lambda t: {"grp": layer ^ t}, row)

    def sum_end(buffer, turn, copies):
        for copy in copies:
            copy.wait()
        return jnp.sum(buffer[turn], axis=0)

    def place(slot, blocks, meta):
        home = lax.rem(peers[slot] + RING - 1, RING) * ROWS + first_row
        found = jnp.int32(0)
        for j in range(RING):
            local = rows_ref[0, j] - home
            found = jnp.where((local >= 0) & (local < ROWS), j * ROWS + local, found)
        source = found // ROWS
        blocks[slot] = coeff[source]
        meta[slot, 0:1] = scale32[pl.ds(source, 1), :]
        meta[slot, 1:2] = jnp.full((1, BS), lax.rem(found, ROWS), jnp.int32).astype(jnp.float32)

    def send_block(slot):
        place(slot, stage, stage_meta)
        copies = []
        for source, target, out, into in (
            (stage_meta, arrived_meta, meta_send, meta_recv),
            (stage, arrived, send_sem, recv_sem),
        ):
            copy = pltpu.make_async_remote_copy(
                src_ref=source.at[slot],
                dst_ref=target.at[slot],
                send_sem=out.at[slot],
                recv_sem=into.at[slot],
                device_id=on_col(peers[slot]),
                device_id_type=MESH,
            )
            copy.start()
            copies.append(copy)
        return copies

    load.wait()
    place(0, arrived, arrived_meta)
    pl.semaphore_wait(barrier, RING - 1 + LAYERS - 1)
    sends = []
    for slot in range(1, EARLY):
        sends += send_block(slot)
    load_precond.wait()
    rhs = rhs_ref[...]
    smooth0 = apply_precond(rhs)
    halo_copies = send_halo(0, smooth0)
    for slot in range(EARLY, RING):
        sends += send_block(slot)

    def batch(first, count):
        for i in range(count):
            slot = first + i

            @pl.when(slot > 0)
            def _():
                for source, target, out, into in (
                    (stage_meta, arrived_meta, meta_send, meta_recv),
                    (stage, arrived, send_sem, recv_sem),
                ):
                    pltpu.make_async_remote_copy(
                        src_ref=source.at[slot],
                        dst_ref=target.at[slot],
                        send_sem=out.at[slot],
                        recv_sem=into.at[slot],
                        device_id=on_col(after),
                        device_id_type=MESH,
                    ).wait_recv()

            blocks = arrived[slot].reshape(WIDE, BS)
            scaled = blocks.astype(jnp.float32) * arrived_meta[slot, 0:1]
            high = scaled.astype(jnp.bfloat16)
            low = (scaled - high.astype(jnp.float32)).astype(jnp.bfloat16)
            products[i] = lax.dot_general(
                jnp.concatenate([high, low], axis=1),
                jnp.concatenate([blocks, blocks], axis=1),
                (((1,), (1,)), ((), ())),
                preferred_element_type=jnp.float32,
            )
        rows_at = [
            jnp.broadcast_to(arrived_meta[first + i, 1:2], (8, BS)) for i in range(count)
        ]
        masks = [
            [jnp.where(at == float(row), 1.0, 0.0) for at in rows_at] for row in range(ROWS)
        ]

        def add(chunk, inner):
            at = pl.ds(pl.multiple_of(chunk * 8, 8), 8)
            for k in range(3):
                lanes = slice(k * BS, (k + 1) * BS)
                these = [products[i, at, lanes] for i in range(count)]
                for row in range(ROWS):
                    gained = masks[row][0] * these[0]
                    for i in range(1, count):
                        gained += masks[row][i] * these[i]
                    total[row, at, lanes] = total[row, at, lanes] + gained
            return inner

        lax.fori_loop(0, WIDE // 8, add, 0)

    def full_batch(number, carry):
        batch(number * BATCH, BATCH)
        return carry

    total[...] = jnp.zeros_like(total)
    lax.fori_loop(0, RING // BATCH // 2, full_batch, 0)
    for copy in halo_copies:
        copy.wait()
    widen(0)
    lax.fori_loop(RING // BATCH // 2, RING // BATCH - 1, full_batch, 0)
    batch(RING - 4, 2)
    batch(RING - 2, 2)

    own_copies = [
        pltpu.make_async_copy(total.at[row, BS : 2 * BS], own_hbm.at[row], out_sem.at[row])
        for row in range(ROWS)
    ]
    for copy in own_copies:
        copy.start()
    slab_copies = []

    def encode(row):
        for way, k, peer in ((1, 2, ahead), (0, 0, before)):
            slab = total[row, k * BS : (k + 1) * BS, :]
            step = jnp.max(jnp.abs(slab), axis=0, keepdims=True) * (1.0 / LEVELS)
            steps[way, row : row + 1, :] = step
            inverse = jnp.where(step > 0.0, 1.0 / step, 0.0)
            scaled = jnp.clip(jnp.round(slab * inverse), -LEVELS, LEVELS)
            codes[way, row] = scaled.astype(jnp.int32).astype(jnp.int16)
            copy = pltpu.make_async_remote_copy(
                src_ref=codes.at[way, row],
                dst_ref=codes_in.at[way, row],
                send_sem=code_send.at[way, row],
                recv_sem=code_recv.at[way, row],
                device_id=on_col(peer),
                device_id_type=MESH,
            )
            copy.start()
            slab_copies.append(copy)

    apply_normal(0)
    part_copies = send_part(0)
    slabs = ((1, 0), (0, 1), (2, 2))
    inner0 = sum(halo[0, way] * part[0, k] for way, k in slabs)
    inner0 += REGULAR * smooth0 * smooth0
    plane_copies = plane_start(0, [rhs * smooth0, inner0])
    for row in range(0, 3):
        encode(row)
    for copy in part_copies:
        copy.wait()
    mapped0 = part[0, 1] + part_in[0, 0] + part_in[0, 1] + REGULAR * smooth0
    smooth_mapped = apply_precond(mapped0)
    halo_copies = send_halo(1, smooth_mapped)
    for row in range(3, 5):
        encode(row)
    row0 = sum_end(red_p, 0, plane_copies)
    layers_copies = layers_start(0, row0)
    rho_here, curve_here = out_of_lanes(row0, 2)
    guess = jnp.where(curve_here > 0.0, rho_here / curve_here, 0.0)
    near_residual = rhs - guess * mapped0
    near_smooth = smooth0 - guess * smooth_mapped
    for copy in halo_copies:
        copy.wait()
    widen(1)
    apply_normal(1)
    part_copies = send_part(1)
    moments = [
        near_residual * near_smooth,
        near_residual * smooth_mapped + mapped0 * near_smooth,
        mapped0 * smooth_mapped,
        REGULAR * near_smooth * near_smooth,
        REGULAR * 2.0 * near_smooth * smooth_mapped,
        REGULAR * smooth_mapped * smooth_mapped,
        REGULAR * near_smooth * smooth0,
        REGULAR * smooth_mapped * smooth0,
    ]
    for way, k in slabs:
        other = halo[1, way]
        here = halo[0, way] - guess * other
        near_part = part[0, k] - guess * part[1, k]
        moments[3] += here * near_part
        moments[4] += here * part[1, k] + other * near_part
        moments[5] += other * part[1, k]
        moments[6] += here * part[0, k]
        moments[7] += other * part[0, k]
    plane_copies = plane_start(1, moments)
    for row in range(5, ROWS):
        encode(row)
    for way, peer in ((1, ahead), (0, before)):
        copy = pltpu.make_async_remote_copy(
            src_ref=steps.at[way],
            dst_ref=steps_in.at[way],
            send_sem=step_send.at[way],
            recv_sem=step_recv.at[way],
            device_id=on_col(peer),
            device_id_type=MESH,
        )
        copy.start()
        slab_copies.append(copy)
    rho0, curve0 = out_of_lanes(sum_end(red_z, 0, layers_copies), 2)
    step0 = rho0 / curve0
    rest = step0 - guess
    residual1 = rhs - step0 * mapped0
    smooth1 = smooth0 - step0 * smooth_mapped
    for copy in part_copies:
        copy.wait()
    mapped_smooth = part[1, 1] + part_in[1, 0] + part_in[1, 1] + REGULAR * smooth_mapped
    sums = out_of_lanes(sum_end(red_p, 1, plane_copies), 8)
    row1 = in_lanes(
        [
            sums[0] - rest * sums[1] + rest * rest * sums[2],
            sums[3] - rest * sums[4] + rest * rest * sums[5],
            sums[6] - rest * sums[7],
        ]
    )
    row1 = sum_end(red_z, 1, layers_start(1, row1))
    rho1, curve11, curve10 = out_of_lanes(row1, 3)
    ratio = rho1 / rho0
    step1 = rho1 / (curve11 + 2.0 * ratio * curve10 + ratio * ratio * curve0)
    mapped1 = (mapped0 - step0 * mapped_smooth) + ratio * mapped0
    vectors[0] = step0 * smooth0 + step1 * (smooth1 + ratio * smooth0)
    vectors[1] = residual1 - step1 * mapped1
    vectors_copy = pltpu.make_async_copy(vectors, vectors_hbm, load_sem.at[0])
    vectors_copy.start()

    for copy in slab_copies:
        copy.wait()
    for copy in own_copies:
        copy.wait()
    for copy in sends:
        copy.wait_send()
    vectors_copy.wait()


def finish(
    codes_hbm,
    steps_hbm,
    own_hbm,
    vectors_hbm,
    normal_hbm,
    x_hbm,
    r_hbm,
    codes,
    steps,
    own,
    vectors,
    normal,
    load_sem,
    small_sem,
    out_sem,
):
    loads = [
        [
            pltpu.make_async_copy(codes_hbm.at[0, row], codes.at[0, row], load_sem.at[0, row]),
            pltpu.make_async_copy(codes_hbm.at[1, row], codes.at[1, row], load_sem.at[1, row]),
            pltpu.make_async_copy(own_hbm.at[row], own.at[row], load_sem.at[2, row]),
        ]
        for row in range(ROWS)
    ]
    load_steps = pltpu.make_async_copy(steps_hbm, steps, small_sem.at[0])
    load_vectors = pltpu.make_async_copy(vectors_hbm, vectors, small_sem.at[1])
    load_steps.start()
    for copies in loads:
        for copy in copies:
            copy.start()
    load_vectors.start()
    rows_in = lax.broadcasted_iota(jnp.int32, (BS, BS), 0)
    columns_in = lax.broadcasted_iota(jnp.int32, (BS, BS), 1)
    diagonal = jnp.where(rows_in == columns_in, REGULAR, 0.0)
    outs = []
    load_steps.wait()
    for row in range(ROWS):
        for copy in loads[row]:
            copy.wait()

        def block(way, l):
            lanes = slice(l * BS, (l + 1) * BS)
            levels = codes[way, row, :, lanes].astype(jnp.int32).astype(jnp.float32)
            return levels * steps[way, row : row + 1, lanes]

        normal[row, 0] = own[row, :, BS : 2 * BS] + diagonal + block(0, 0) + block(1, 2)
        normal[row, 1] = block(0, 1)
        normal[row, 2] = own[row, :, 0:BS]
        normal[row, 3] = own[row, :, 2 * BS :]
        normal[row, 4] = block(1, 1)
        normal[row, 5] = block(0, 2)
        normal[row, 6] = block(1, 0)
        out = pltpu.make_async_copy(normal.at[row], normal_hbm.at[row], out_sem.at[row])
        out.start()
        outs.append(out)
    load_vectors.wait()
    for which, target in enumerate((x_hbm, r_hbm)):
        out = pltpu.make_async_copy(vectors.at[which], target, small_sem.at[2 + which])
        out.start()
        outs.append(out)
    for out in outs:
        out.wait()


def on_device(coeff, scaling, block_rows, precond, rhs):
    f32, bf16 = jnp.float32, jnp.bfloat16
    anywhere = pl.BlockSpec(memory_space=pl.ANY)
    dma = pltpu.SemaphoreType.DMA
    codes, steps, own, vectors = pl.pallas_call(
        kernel,
        out_shape=(
            jax.ShapeDtypeStruct((2, ROWS, BS, WIDE), jnp.int16),
            jax.ShapeDtypeStruct((2, ROWS, WIDE), f32),
            jax.ShapeDtypeStruct((ROWS, BS, WIDE), f32),
            jax.ShapeDtypeStruct((2, ROWS, BS), f32),
        ),
        in_specs=[anywhere] * 5,
        out_specs=(anywhere,) * 4,
        scratch_shapes=[
            pltpu.VMEM((RING, 3, BS, BS), bf16),
            pltpu.SMEM((3, RING), jnp.int32),
            pltpu.VMEM((RING, BS), bf16),
            pltpu.VMEM((ROWS, BS), f32),
            pltpu.VMEM((RING, BS), f32),
            pltpu.VMEM((RING, 3, BS, BS), bf16),
            pltpu.VMEM((RING, 2, BS), f32),
            pltpu.VMEM((RING, 3, BS, BS), bf16),
            pltpu.VMEM((RING, 2, BS), f32),
            pltpu.VMEM((BATCH, WIDE, WIDE), f32),
            pltpu.VMEM((ROWS, WIDE, WIDE), f32),
            pltpu.VMEM((ROWS, BS, BS), f32),
            pltpu.VMEM((ROWS, WIDE, BS), f32),
            pltpu.VMEM((ROWS, BS, BS), f32),
            pltpu.VMEM((2, 3, ROWS, BS), f32),
            pltpu.VMEM((2, 3, ROWS, BS), f32),
            pltpu.VMEM((2, 2, ROWS, BS), f32),
            pltpu.VMEM((2, ROWS, BS, WIDE), jnp.int16),
            pltpu.VMEM((2, ROWS, WIDE), f32),
            pltpu.VMEM((2, ROWS, BS), f32),
            pltpu.VMEM((2, LAYERS, 1, BS), f32),
            pltpu.VMEM((2, RING, 1, BS), f32),
            dma((5,)),
            dma((RING,)),
            dma((RING,)),
            dma((RING,)),
            dma((RING,)),
            dma((2, 3)),
            dma((2, 3)),
            dma((2, 2)),
            dma((2, 2)),
            dma((2, ROWS)),
            dma((2, ROWS)),
            dma((2,)),
            dma((2,)),
            dma((2, LAYERS + RING)),
            dma((2, LAYERS + RING)),
            dma((ROWS,)),
        ],
        compiler_params=pltpu.CompilerParams(
            collective_id=0, has_side_effects=True, vmem_limit_bytes=56 << 20
        ),
    )(coeff, scaling, block_rows.T, precond, rhs)
    return pl.pallas_call(
        finish,
        out_shape=(
            jax.ShapeDtypeStruct((ROWS, 7, BS, BS), f32),
            jax.ShapeDtypeStruct((ROWS, BS), f32),
            jax.ShapeDtypeStruct((ROWS, BS), f32),
        ),
        in_specs=[anywhere] * 4,
        out_specs=(anywhere,) * 3,
        scratch_shapes=[
            pltpu.VMEM((2, ROWS, BS, WIDE), jnp.int16),
            pltpu.VMEM((2, ROWS, WIDE), f32),
            pltpu.VMEM((ROWS, BS, WIDE), f32),
            pltpu.VMEM((2, ROWS, BS), f32),
            pltpu.VMEM((ROWS, 7, BS, BS), f32),
            dma((3, ROWS)),
            dma((4,)),
            dma((ROWS,)),
        ],
        compiler_params=pltpu.CompilerParams(vmem_limit_bytes=56 << 20),
    )(codes, steps, own, vectors)


def solution(mesh):
    whole = P(("grp", "col"))
    return jax.shard_map(
        on_device,
        mesh=mesh,
        in_specs=(whole,) * 5,
        out_specs=(whole,) * 3,
        check_vma=False,
    )
```

```python
import jax
import jax.numpy as jnp
from jax import lax
from jax.experimental import pallas as pl
from jax.experimental.pallas import tpu as pltpu
from jax.sharding import PartitionSpec as P

MESH = pl.DeviceIdType.MESH
RING = 32
ROWS = 8
BS = 128
WIDE = 3 * BS
LAYERS = 8
BATCH = 4
EARLY = 9
REGULAR = 0.5
LEVELS = 32767.0

_GROUPS = (
    ((1, 0), (3, 0), (0, 1), (0, 3)),
    ((2, 0), (0, 2)),
    ((1, 1), (3, 3)),
    ((1, 3), (3, 1)),
    ((2, 1), (2, 3), (1, 2), (3, 2)),
    ((2, 2),),
)
MOVES = [(0, 0, 0), (0, 0, 1)] + [
    (dx, dy, dc) for group in _GROUPS for dc in (0, 1) for dx, dy in group
]


def moved(me, move):
    dx, dy, dc = move
    return (
        lax.rem(me // 8 + dx, 4) * 8
        + lax.rem(lax.rem(me // 2, 4) + dy, 4) * 2
        + lax.rem(me + dc, 2)
    )


def on_col(index):
    return {"col": index}


def spread(columns, first, out, lead):
    out[lead] = jnp.broadcast_to(columns[:, first : first + 1], (BS, BS))


def kernel(
    coeff_hbm,
    scaling_hbm,
    rows_hbm,
    precond_hbm,
    rhs_hbm,
    codes_in,
    steps_in,
    own_hbm,
    vectors_hbm,
    coeff,
    rows_ref,
    scaling_ref,
    rhs_ref,
    scale32,
    stage,
    stage_meta,
    arrived,
    arrived_meta,
    products,
    total,
    precond,
    wide,
    wide_own,
    halo,
    part,
    part_in,
    codes,
    steps,
    vectors,
    red_z,
    red_p,
    load_sem,
    send_sem,
    recv_sem,
    meta_send,
    meta_recv,
    halo_send,
    halo_recv,
    part_send,
    part_recv,
    code_send,
    code_recv,
    step_send,
    step_recv,
    red_send,
    red_recv,
    out_sem,
):
    me = lax.axis_index("col")
    layer = lax.axis_index("grp")
    before, after = lax.rem(me + RING - 1, RING), lax.rem(me + 1, RING)
    ahead, behind = lax.rem(me + 2, RING), lax.rem(me + RING - 2, RING)
    peers = [moved(me, move) for move in MOVES]

    load = pltpu.make_async_copy(coeff_hbm, coeff, load_sem.at[0])
    load.start()
    barrier = pltpu.get_barrier_semaphore()
    for other in (4, 3, 5, 2, 6, 1, 7):
        pl.semaphore_signal(
            barrier,
            inc=1,
            device_id={"grp": lax.rem(layer + other, LAYERS)},
            device_id_type=MESH,
        )
    for peer in peers[:0:-1]:
        pl.semaphore_signal(barrier, inc=1, device_id=on_col(peer), device_id_type=MESH)
    small_loads = [
        pltpu.make_async_copy(source, target, load_sem.at[2 + i])
        for i, (source, target) in enumerate(
            ((rows_hbm, rows_ref), (scaling_hbm, scaling_ref), (rhs_hbm, rhs_ref))
        )
    ]
    for copy in small_loads:
        copy.start()
    load_precond = pltpu.make_async_copy(precond_hbm, precond, load_sem.at[1])
    load_precond.start()
    for copy in small_loads:
        copy.wait()

    scale32[...] = scaling_ref[...].astype(jnp.float32)
    first_row = layer * (RING * ROWS)

    def transposed(pieces):
        rows = [*pieces, jnp.zeros((BS - ROWS * len(pieces), BS), jnp.float32)]
        return jnp.transpose(jnp.concatenate(rows, axis=0))

    def apply_precond(vector):
        columns = transposed([vector])
        for row in range(ROWS):
            spread(columns, row, wide_own, row)
        outs = []
        for row in range(ROWS):
            acc = jnp.zeros((8, BS), jnp.float32)
            for chunk in range(0, BS, 8):
                acc += precond[row, chunk : chunk + 8, :] * wide_own[row, chunk : chunk + 8, :]
            outs.append(jnp.sum(acc, axis=0, keepdims=True))
        return jnp.concatenate(outs, axis=0)

    def send_halo(turn, vector):
        halo[turn, 0] = vector
        copies = []
        for way, peer in ((1, after), (2, behind)):
            copy = pltpu.make_async_remote_copy(
                src_ref=halo.at[turn, 0],
                dst_ref=halo.at[turn, way],
                send_sem=halo_send.at[turn, way],
                recv_sem=halo_recv.at[turn, way],
                device_id=on_col(peer),
                device_id_type=MESH,
            )
            copy.start()
            copies.append(copy)
        return copies

    def widen(turn, slabs):
        columns = transposed([halo[turn, way] for way, _ in slabs])
        for row in range(ROWS):
            for i, (_, k) in enumerate(slabs):
                wide[row, k * BS : (k + 1) * BS, :] = jnp.broadcast_to(
                    columns[:, i * ROWS + row : i * ROWS + row + 1], (BS, BS)
                )

    def apply_normal(turn, slabs, fresh):
        def one(row, carry):
            acc = [jnp.zeros((8, BS), jnp.float32) for _ in range(3)]
            for _, k in slabs:
                for chunk in range(k * BS, (k + 1) * BS, 8):
                    v = wide[row, chunk : chunk + 8, :]
                    for l in range(3):
                        acc[l] += total[row, chunk : chunk + 8, l * BS : (l + 1) * BS] * v
            for l in range(3):
                gained = jnp.sum(acc[l], axis=0, keepdims=True)
                if not fresh:
                    gained += part[turn, l, pl.ds(row, 1), :]
                part[turn, l, pl.ds(row, 1), :] = gained
            return carry

        lax.fori_loop(0, ROWS, one, 0)

    def send_part(turn):
        copies = []
        for k, way, peer in ((0, 0, before), (2, 1, ahead)):
            copy = pltpu.make_async_remote_copy(
                src_ref=part.at[turn, k],
                dst_ref=part_in.at[turn, way],
                send_sem=part_send.at[turn, way],
                recv_sem=part_recv.at[turn, way],
                device_id=on_col(peer),
                device_id_type=MESH,
            )
            copy.start()
            copies.append(copy)
        return copies

    slabs = ((1, 0), (0, 1), (2, 2))

    lane = lax.broadcasted_iota(jnp.int32, (1, BS), 1)

    def in_lanes(scalars):
        row = jnp.zeros((1, BS), jnp.float32)
        for i, scalar in enumerate(scalars):
            row = jnp.where(lane == i, scalar, row)
        return row

    def out_of_lanes(row, count):
        return [jnp.sum(jnp.where(lane == i, row, 0.0), keepdims=True) for i in range(count)]

    def gather(buffer, turn, base, count, target, value):
        buffer[turn, 0] = value
        copies = []
        for t in range(1, count):
            copy = pltpu.make_async_remote_copy(
                src_ref=buffer.at[turn, 0],
                dst_ref=buffer.at[turn, t],
                send_sem=red_send.at[turn, base + t],
                recv_sem=red_recv.at[turn, base + t],
                device_id=target(t),
                device_id_type=MESH,
            )
            copy.start()
            copies.append(copy)
        return copies

    def plane_start(turn, values):
        row = in_lanes([jnp.sum(v, keepdims=True) for v in values])
        return gather(red_p, turn, LAYERS, RING, lambda t: {"col": me ^ t}, row)

    def layers_start(turn, row):
        return gather(red_z, turn, 0, LAYERS, lambda t: {"grp": layer ^ t}, row)

    def sum_end(buffer, turn, copies):
        for copy in copies:
            copy.wait()
        return jnp.sum(buffer[turn], axis=0)

    def place(slot, blocks, meta):
        home = lax.rem(peers[slot] + RING - 1, RING) * ROWS + first_row
        found = jnp.int32(0)
        for j in range(RING):
            local = rows_ref[0, j] - home
            found = jnp.where((local >= 0) & (local < ROWS), j * ROWS + local, found)
        source = found // ROWS
        blocks[slot] = coeff[source]
        meta[slot, 0:1] = scale32[pl.ds(source, 1), :]
        meta[slot, 1:2] = jnp.full((1, BS), lax.rem(found, ROWS), jnp.int32).astype(jnp.float32)

    def send_block(slot):
        place(slot, stage, stage_meta)
        copies = []
        for source, target, out, into in (
            (stage_meta, arrived_meta, meta_send, meta_recv),
            (stage, arrived, send_sem, recv_sem),
        ):
            copy = pltpu.make_async_remote_copy(
                src_ref=source.at[slot],
                dst_ref=target.at[slot],
                send_sem=out.at[slot],
                recv_sem=into.at[slot],
                device_id=on_col(peers[slot]),
                device_id_type=MESH,
            )
            copy.start()
            copies.append(copy)
        return copies

    load.wait()
    place(0, arrived, arrived_meta)
    pl.semaphore_wait(barrier, RING - 1 + LAYERS - 1)
    sends = []
    for slot in range(1, EARLY):
        sends += send_block(slot)
    load_precond.wait()
    rhs = rhs_ref[...]
    smooth0 = apply_precond(rhs)
    halo_copies = send_halo(0, smooth0)
    for slot in range(EARLY, RING):
        sends += send_block(slot)

    def multiply(first, count):
        for i in range(count):
            slot = first + i

            @pl.when(slot > 0)
            def _():
                for source, target, out, into in (
                    (stage_meta, arrived_meta, meta_send, meta_recv),
                    (stage, arrived, send_sem, recv_sem),
                ):
                    pltpu.make_async_remote_copy(
                        src_ref=source.at[slot],
                        dst_ref=target.at[slot],
                        send_sem=out.at[slot],
                        recv_sem=into.at[slot],
                        device_id=on_col(after),
                        device_id_type=MESH,
                    ).wait_recv()

            blocks = arrived[slot].reshape(WIDE, BS)
            scaled = blocks.astype(jnp.float32) * arrived_meta[slot, 0:1]
            high = scaled.astype(jnp.bfloat16)
            low = (scaled - high.astype(jnp.float32)).astype(jnp.bfloat16)
            products[i] = lax.dot_general(
                jnp.concatenate([high, low], axis=1),
                jnp.concatenate([blocks, blocks], axis=1),
                (((1,), (1,)), ((), ())),
                preferred_element_type=jnp.float32,
            )

    def row_masks(slot):
        at = jnp.broadcast_to(arrived_meta[slot, 1:2], (8, BS))
        return [jnp.where(at == float(row), 1.0, 0.0) for row in range(ROWS)]

    def accumulate(first, count):
        masks = list(zip(*[row_masks(first + i) for i in range(count)]))

        def add(chunk, inner):
            at = pl.ds(pl.multiple_of(chunk * 8, 8), 8)
            for k in range(3):
                lanes = slice(k * BS, (k + 1) * BS)
                these = [products[i, at, lanes] for i in range(count)]
                for row in range(ROWS):
                    gained = masks[row][0] * these[0]
                    for i in range(1, count):
                        gained += masks[row][i] * these[i]
                    total[row, at, lanes] = total[row, at, lanes] + gained
            return inner

        lax.fori_loop(0, WIDE // 8, add, 0)

    def full_batch(number, carry):
        multiply(number * BATCH, BATCH)
        accumulate(number * BATCH, BATCH)
        return carry

    def correct(slot, i):
        masks = row_masks(slot)
        acc = [jnp.zeros((8, BS), jnp.float32) for _ in range(3)]
        for chunk in range(0, WIDE, 8):
            v = masks[0] * wide[0, chunk : chunk + 8, :]
            for row in range(1, ROWS):
                v += masks[row] * wide[row, chunk : chunk + 8, :]
            for l in range(3):
                acc[l] += products[i, chunk : chunk + 8, l * BS : (l + 1) * BS] * v
        rows_in = lax.broadcasted_iota(jnp.int32, (ROWS, BS), 0).astype(jnp.float32)
        here = rows_in == arrived_meta[slot, 1:2]
        for l in range(3):
            part[0, l] += jnp.where(here, jnp.sum(acc[l], axis=0, keepdims=True), 0.0)

    total[...] = jnp.zeros_like(total)
    lax.fori_loop(0, RING // BATCH // 2, full_batch, 0)
    for copy in halo_copies:
        copy.wait()
    widen(0, slabs)
    lax.fori_loop(RING // BATCH // 2, RING // BATCH - 1, full_batch, 0)
    multiply(RING - 4, 2)
    accumulate(RING - 4, 2)
    apply_normal(0, slabs, True)
    multiply(RING - 2, 2)
    correct(RING - 2, 0)
    correct(RING - 1, 1)
    part_copies = send_part(0)
    inner0 = sum(halo[0, way] * part[0, k] for way, k in slabs)
    inner0 += REGULAR * smooth0 * smooth0
    plane_copies = plane_start(0, [rhs * smooth0, inner0])
    accumulate(RING - 2, 2)

    own_copies = [
        pltpu.make_async_copy(total.at[row, BS : 2 * BS], own_hbm.at[row], out_sem.at[row])
        for row in range(ROWS)
    ]
    for copy in own_copies:
        copy.start()
    slab_copies = []

    def encode(row):
        for way, k, peer in ((1, 2, ahead), (0, 0, before)):
            slab = total[row, k * BS : (k + 1) * BS, :]
            step = jnp.max(jnp.abs(slab), axis=0, keepdims=True) * (1.0 / LEVELS)
            steps[way, row : row + 1, :] = step
            inverse = jnp.where(step > 0.0, 1.0 / step, 0.0)
            scaled = jnp.clip(jnp.round(slab * inverse), -LEVELS, LEVELS)
            codes[way, row] = scaled.astype(jnp.int32).astype(jnp.int16)
            copy = pltpu.make_async_remote_copy(
                src_ref=codes.at[way, row],
                dst_ref=codes_in.at[way, row],
                send_sem=code_send.at[way, row],
                recv_sem=code_recv.at[way, row],
                device_id=on_col(peer),
                device_id_type=MESH,
            )
            copy.start()
            slab_copies.append(copy)

    for row in range(0, 2):
        encode(row)
    for copy in part_copies:
        copy.wait()
    mapped0 = part[0, 1] + part_in[0, 0] + part_in[0, 1] + REGULAR * smooth0
    smooth_mapped = apply_precond(mapped0)
    halo_copies = send_halo(1, smooth_mapped)
    for row in range(2, 4):
        encode(row)
    widen(1, slabs[1:2])
    apply_normal(1, slabs[1:2], True)
    row0 = sum_end(red_p, 0, plane_copies)
    layers_copies = layers_start(0, row0)
    rho_here, curve_here = out_of_lanes(row0, 2)
    guess = jnp.where(curve_here > 0.0, rho_here / curve_here, 0.0)
    near_residual = rhs - guess * mapped0
    near_smooth = smooth0 - guess * smooth_mapped
    for copy in halo_copies:
        copy.wait()
    widen(1, slabs[::2])
    apply_normal(1, slabs[::2], False)
    part_copies = send_part(1)
    moments = [
        near_residual * near_smooth,
        near_residual * smooth_mapped + mapped0 * near_smooth,
        mapped0 * smooth_mapped,
        REGULAR * near_smooth * near_smooth,
        REGULAR * 2.0 * near_smooth * smooth_mapped,
        REGULAR * smooth_mapped * smooth_mapped,
        REGULAR * near_smooth * smooth0,
        REGULAR * smooth_mapped * smooth0,
    ]
    for way, k in slabs:
        other = halo[1, way]
        here = halo[0, way] - guess * other
        near_part = part[0, k] - guess * part[1, k]
        moments[3] += here * near_part
        moments[4] += here * part[1, k] + other * near_part
        moments[5] += other * part[1, k]
        moments[6] += here * part[0, k]
        moments[7] += other * part[0, k]
    plane_copies = plane_start(1, moments)
    for row in range(4, ROWS):
        encode(row)
    for way, peer in ((1, ahead), (0, before)):
        copy = pltpu.make_async_remote_copy(
            src_ref=steps.at[way],
            dst_ref=steps_in.at[way],
            send_sem=step_send.at[way],
            recv_sem=step_recv.at[way],
            device_id=on_col(peer),
            device_id_type=MESH,
        )
        copy.start()
        slab_copies.append(copy)
    rho0, curve0 = out_of_lanes(sum_end(red_z, 0, layers_copies), 2)
    step0 = rho0 / curve0
    rest = step0 - guess
    residual1 = rhs - step0 * mapped0
    smooth1 = smooth0 - step0 * smooth_mapped
    for copy in part_copies:
        copy.wait()
    mapped_smooth = part[1, 1] + part_in[1, 0] + part_in[1, 1] + REGULAR * smooth_mapped
    powers = in_lanes([1.0, -rest, rest * rest, 1.0, -rest, rest * rest, 1.0, -rest])
    row1 = sum_end(red_p, 1, plane_copies) * powers
    row1 = sum_end(red_z, 1, layers_start(1, row1))
    rho1, curve11, curve10 = (
        jnp.sum(jnp.where((lane >= first) & (lane < last), row1, 0.0), keepdims=True)
        for first, last in ((0, 3), (3, 6), (6, 8))
    )
    ratio = rho1 / rho0
    step1 = rho1 / (curve11 + 2.0 * ratio * curve10 + ratio * ratio * curve0)
    mapped1 = (mapped0 - step0 * mapped_smooth) + ratio * mapped0
    vectors[0] = step0 * smooth0 + step1 * (smooth1 + ratio * smooth0)
    vectors[1] = residual1 - step1 * mapped1
    vectors_copy = pltpu.make_async_copy(vectors, vectors_hbm, load_sem.at[0])
    vectors_copy.start()

    for copy in slab_copies:
        copy.wait()
    for copy in own_copies:
        copy.wait()
    for copy in sends:
        copy.wait_send()
    vectors_copy.wait()


def finish(
    codes_hbm,
    steps_hbm,
    own_hbm,
    vectors_hbm,
    normal_hbm,
    x_hbm,
    r_hbm,
    codes,
    steps,
    own,
    vectors,
    normal,
    load_sem,
    small_sem,
    out_sem,
):
    loads = [
        [
            pltpu.make_async_copy(codes_hbm.at[0, row], codes.at[0, row], load_sem.at[0, row]),
            pltpu.make_async_copy(codes_hbm.at[1, row], codes.at[1, row], load_sem.at[1, row]),
            pltpu.make_async_copy(own_hbm.at[row], own.at[row], load_sem.at[2, row]),
        ]
        for row in range(ROWS)
    ]
    load_steps = pltpu.make_async_copy(steps_hbm, steps, small_sem.at[0])
    load_vectors = pltpu.make_async_copy(vectors_hbm, vectors, small_sem.at[1])
    load_steps.start()
    for copies in loads:
        for copy in copies:
            copy.start()
    load_vectors.start()
    rows_in = lax.broadcasted_iota(jnp.int32, (BS, BS), 0)
    columns_in = lax.broadcasted_iota(jnp.int32, (BS, BS), 1)
    diagonal = jnp.where(rows_in == columns_in, REGULAR, 0.0)
    outs = []
    load_steps.wait()
    for row in range(ROWS):
        for copy in loads[row]:
            copy.wait()

        def block(way, l):
            lanes = slice(l * BS, (l + 1) * BS)
            levels = codes[way, row, :, lanes].astype(jnp.int32).astype(jnp.float32)
            return levels * steps[way, row : row + 1, lanes]

        normal[row, 0] = own[row, :, BS : 2 * BS] + diagonal + block(0, 0) + block(1, 2)
        normal[row, 1] = block(0, 1)
        normal[row, 2] = own[row, :, 0:BS]
        normal[row, 3] = own[row, :, 2 * BS :]
        normal[row, 4] = block(1, 1)
        normal[row, 5] = block(0, 2)
        normal[row, 6] = block(1, 0)
        out = pltpu.make_async_copy(normal.at[row], normal_hbm.at[row], out_sem.at[row])
        out.start()
        outs.append(out)
    load_vectors.wait()
    for which, target in enumerate((x_hbm, r_hbm)):
        out = pltpu.make_async_copy(vectors.at[which], target, small_sem.at[2 + which])
        out.start()
        outs.append(out)
    for out in outs:
        out.wait()


def on_device(coeff, scaling, block_rows, precond, rhs):
    f32, bf16 = jnp.float32, jnp.bfloat16
    anywhere = pl.BlockSpec(memory_space=pl.ANY)
    dma = pltpu.SemaphoreType.DMA
    codes, steps, own, vectors = pl.pallas_call(
        kernel,
        out_shape=(
            jax.ShapeDtypeStruct((2, ROWS, BS, WIDE), jnp.int16),
            jax.ShapeDtypeStruct((2, ROWS, WIDE), f32),
            jax.ShapeDtypeStruct((ROWS, BS, WIDE), f32),
            jax.ShapeDtypeStruct((2, ROWS, BS), f32),
        ),
        in_specs=[anywhere] * 5,
        out_specs=(anywhere,) * 4,
        scratch_shapes=[
            pltpu.VMEM((RING, 3, BS, BS), bf16),
            pltpu.SMEM((3, RING), jnp.int32),
            pltpu.VMEM((RING, BS), bf16),
            pltpu.VMEM((ROWS, BS), f32),
            pltpu.VMEM((RING, BS), f32),
            pltpu.VMEM((RING, 3, BS, BS), bf16),
            pltpu.VMEM((RING, 2, BS), f32),
            pltpu.VMEM((RING, 3, BS, BS), bf16),
            pltpu.VMEM((RING, 2, BS), f32),
            pltpu.VMEM((BATCH, WIDE, WIDE), f32),
            pltpu.VMEM((ROWS, WIDE, WIDE), f32),
            pltpu.VMEM((ROWS, BS, BS), f32),
            pltpu.VMEM((ROWS, WIDE, BS), f32),
            pltpu.VMEM((ROWS, BS, BS), f32),
            pltpu.VMEM((2, 3, ROWS, BS), f32),
            pltpu.VMEM((2, 3, ROWS, BS), f32),
            pltpu.VMEM((2, 2, ROWS, BS), f32),
            pltpu.VMEM((2, ROWS, BS, WIDE), jnp.int16),
            pltpu.VMEM((2, ROWS, WIDE), f32),
            pltpu.VMEM((2, ROWS, BS), f32),
            pltpu.VMEM((2, LAYERS, 1, BS), f32),
            pltpu.VMEM((2, RING, 1, BS), f32),
            dma((5,)),
            dma((RING,)),
            dma((RING,)),
            dma((RING,)),
            dma((RING,)),
            dma((2, 3)),
            dma((2, 3)),
            dma((2, 2)),
            dma((2, 2)),
            dma((2, ROWS)),
            dma((2, ROWS)),
            dma((2,)),
            dma((2,)),
            dma((2, LAYERS + RING)),
            dma((2, LAYERS + RING)),
            dma((ROWS,)),
        ],
        compiler_params=pltpu.CompilerParams(
            collective_id=0, has_side_effects=True, vmem_limit_bytes=56 << 20
        ),
    )(coeff, scaling, block_rows.T, precond, rhs)
    return pl.pallas_call(
        finish,
        out_shape=(
            jax.ShapeDtypeStruct((ROWS, 7, BS, BS), f32),
            jax.ShapeDtypeStruct((ROWS, BS), f32),
            jax.ShapeDtypeStruct((ROWS, BS), f32),
        ),
        in_specs=[anywhere] * 4,
        out_specs=(anywhere,) * 3,
        scratch_shapes=[
            pltpu.VMEM((2, ROWS, BS, WIDE), jnp.int16),
            pltpu.VMEM((2, ROWS, WIDE), f32),
            pltpu.VMEM((ROWS, BS, WIDE), f32),
            pltpu.VMEM((2, ROWS, BS), f32),
            pltpu.VMEM((ROWS, 7, BS, BS), f32),
            dma((3, ROWS)),
            dma((4,)),
            dma((ROWS,)),
        ],
        compiler_params=pltpu.CompilerParams(vmem_limit_bytes=56 << 20),
    )(codes, steps, own, vectors)


def solution(mesh):
    whole = P(("grp", "col"))
    return jax.shard_map(
        on_device,
        mesh=mesh,
        in_specs=(whole,) * 5,
        out_specs=(whole,) * 3,
        check_vma=False,
    )
```

```python
import jax
import jax.numpy as jnp
from jax import lax
from jax.experimental import pallas as pl
from jax.experimental.pallas import tpu as pltpu
from jax.sharding import PartitionSpec as P

MESH = pl.DeviceIdType.MESH
RING = 32
ROWS = 8
BS = 128
WIDE = 3 * BS
LAYERS = 8
BATCH = 4
EARLY = 9
REGULAR = 0.5
LEVELS = 32767.0

_GROUPS = (
    ((1, 0), (3, 0), (0, 1), (0, 3)),
    ((2, 0), (0, 2)),
    ((1, 1), (3, 3)),
    ((1, 3), (3, 1)),
    ((2, 1), (2, 3), (1, 2), (3, 2)),
    ((2, 2),),
)
MOVES = [(0, 0, 0), (0, 0, 1)] + [
    (dx, dy, dc) for group in _GROUPS for dc in (0, 1) for dx, dy in group
]


def moved(me, move):
    dx, dy, dc = move
    return (
        lax.rem(me // 8 + dx, 4) * 8
        + lax.rem(lax.rem(me // 2, 4) + dy, 4) * 2
        + lax.rem(me + dc, 2)
    )


def on_col(index):
    return {"col": index}


def spread(columns, first, out, lead):
    out[lead] = jnp.broadcast_to(columns[:, first : first + 1], (BS, BS))


def kernel(
    coeff_hbm,
    scaling_hbm,
    rows_hbm,
    precond_hbm,
    rhs_hbm,
    codes_in,
    steps_in,
    own_hbm,
    vectors_hbm,
    coeff,
    rows_ref,
    scaling_ref,
    rhs_ref,
    scale32,
    stage,
    stage_meta,
    arrived,
    arrived_meta,
    products,
    total,
    precond,
    wide,
    wide_own,
    halo,
    part,
    part_in,
    codes,
    steps,
    vectors,
    red_z,
    red_p,
    load_sem,
    send_sem,
    recv_sem,
    meta_send,
    meta_recv,
    halo_send,
    halo_recv,
    part_send,
    part_recv,
    code_send,
    code_recv,
    step_send,
    step_recv,
    red_send,
    red_recv,
    out_sem,
):
    me = lax.axis_index("col")
    layer = lax.axis_index("grp")
    before, after = lax.rem(me + RING - 1, RING), lax.rem(me + 1, RING)
    ahead, behind = lax.rem(me + 2, RING), lax.rem(me + RING - 2, RING)
    peers = [moved(me, move) for move in MOVES]

    load = pltpu.make_async_copy(coeff_hbm, coeff, load_sem.at[0])
    load.start()
    barrier = pltpu.get_barrier_semaphore()
    for other in (4, 3, 5, 2, 6, 1, 7):
        pl.semaphore_signal(
            barrier,
            inc=1,
            device_id={"grp": lax.rem(layer + other, LAYERS)},
            device_id_type=MESH,
        )
    for peer in peers[:0:-1]:
        pl.semaphore_signal(barrier, inc=1, device_id=on_col(peer), device_id_type=MESH)
    small_loads = [
        pltpu.make_async_copy(source, target, load_sem.at[2 + i])
        for i, (source, target) in enumerate(
            ((rows_hbm, rows_ref), (scaling_hbm, scaling_ref), (rhs_hbm, rhs_ref))
        )
    ]
    for copy in small_loads:
        copy.start()
    load_precond = pltpu.make_async_copy(precond_hbm, precond, load_sem.at[1])
    load_precond.start()
    for copy in small_loads:
        copy.wait()

    scale32[...] = scaling_ref[...].astype(jnp.float32)
    first_row = layer * (RING * ROWS)

    def transposed(pieces):
        rows = [*pieces, jnp.zeros((BS - ROWS * len(pieces), BS), jnp.float32)]
        return jnp.transpose(jnp.concatenate(rows, axis=0))

    def apply_precond(vector):
        columns = transposed([vector])
        for row in range(ROWS):
            spread(columns, row, wide_own, row)
        outs = []
        for row in range(ROWS):
            acc = jnp.zeros((8, BS), jnp.float32)
            for chunk in range(0, BS, 8):
                acc += precond[row, chunk : chunk + 8, :] * wide_own[row, chunk : chunk + 8, :]
            outs.append(jnp.sum(acc, axis=0, keepdims=True))
        return jnp.concatenate(outs, axis=0)

    def send_halo(turn, vector):
        halo[turn, 0] = vector
        copies = []
        for way, peer in ((1, after), (2, behind)):
            copy = pltpu.make_async_remote_copy(
                src_ref=halo.at[turn, 0],
                dst_ref=halo.at[turn, way],
                send_sem=halo_send.at[turn, way],
                recv_sem=halo_recv.at[turn, way],
                device_id=on_col(peer),
                device_id_type=MESH,
            )
            copy.start()
            copies.append(copy)
        return copies

    def widen(turn, slabs):
        columns = transposed([halo[turn, way] for way, _ in slabs])
        for row in range(ROWS):
            for i, (_, k) in enumerate(slabs):
                wide[row, k * BS : (k + 1) * BS, :] = jnp.broadcast_to(
                    columns[:, i * ROWS + row : i * ROWS + row + 1], (BS, BS)
                )

    def apply_normal(turn, slabs, fresh):
        def one(row, carry):
            acc = [jnp.zeros((8, BS), jnp.float32) for _ in range(3)]
            for _, k in slabs:
                for chunk in range(k * BS, (k + 1) * BS, 8):
                    v = wide[row, chunk : chunk + 8, :]
                    for l in range(3):
                        acc[l] += total[row, chunk : chunk + 8, l * BS : (l + 1) * BS] * v
            for l in range(3):
                gained = jnp.sum(acc[l], axis=0, keepdims=True)
                if not fresh:
                    gained += part[turn, l, pl.ds(row, 1), :]
                part[turn, l, pl.ds(row, 1), :] = gained
            return carry

        lax.fori_loop(0, ROWS, one, 0)

    def send_part(turn):
        copies = []
        for k, way, peer in ((0, 0, before), (2, 1, ahead)):
            copy = pltpu.make_async_remote_copy(
                src_ref=part.at[turn, k],
                dst_ref=part_in.at[turn, way],
                send_sem=part_send.at[turn, way],
                recv_sem=part_recv.at[turn, way],
                device_id=on_col(peer),
                device_id_type=MESH,
            )
            copy.start()
            copies.append(copy)
        return copies

    slabs = ((1, 0), (0, 1), (2, 2))

    lane = lax.broadcasted_iota(jnp.int32, (1, BS), 1)

    def in_lanes(scalars):
        row = jnp.zeros((1, BS), jnp.float32)
        for i, scalar in enumerate(scalars):
            row = jnp.where(lane == i, scalar, row)
        return row

    def out_of_lanes(row, count):
        return [jnp.sum(jnp.where(lane == i, row, 0.0), keepdims=True) for i in range(count)]

    def gather(buffer, turn, base, count, target, value):
        buffer[turn, 0] = value
        copies = []
        for t in range(1, count):
            copy = pltpu.make_async_remote_copy(
                src_ref=buffer.at[turn, 0],
                dst_ref=buffer.at[turn, t],
                send_sem=red_send.at[turn, base + t],
                recv_sem=red_recv.at[turn, base + t],
                device_id=target(t),
                device_id_type=MESH,
            )
            copy.start()
            copies.append(copy)
        return copies

    def plane_start(turn, values):
        row = in_lanes([jnp.sum(v, keepdims=True) for v in values])
        return gather(red_p, turn, LAYERS, RING, lambda t: {"col": me ^ t}, row)

    def layers_start(turn, row):
        return gather(red_z, turn, 0, LAYERS, lambda t: {"grp": layer ^ t}, row)

    def sum_end(buffer, turn, copies):
        for copy in copies:
            copy.wait()
        return jnp.sum(buffer[turn], axis=0)

    def place(slot, blocks, meta):
        home = lax.rem(peers[slot] + RING - 1, RING) * ROWS + first_row
        found = jnp.int32(0)
        for j in range(RING):
            local = rows_ref[0, j] - home
            found = jnp.where((local >= 0) & (local < ROWS), j * ROWS + local, found)
        source = found // ROWS
        blocks[slot] = coeff[source]
        meta[slot, 0:1] = scale32[pl.ds(source, 1), :]
        meta[slot, 1:2] = jnp.full((1, BS), lax.rem(found, ROWS), jnp.int32).astype(jnp.float32)

    def send_block(slot):
        place(slot, stage, stage_meta)
        copies = []
        for source, target, out, into in (
            (stage_meta, arrived_meta, meta_send, meta_recv),
            (stage, arrived, send_sem, recv_sem),
        ):
            copy = pltpu.make_async_remote_copy(
                src_ref=source.at[slot],
                dst_ref=target.at[slot],
                send_sem=out.at[slot],
                recv_sem=into.at[slot],
                device_id=on_col(peers[slot]),
                device_id_type=MESH,
            )
            copy.start()
            copies.append(copy)
        return copies

    load.wait()
    place(0, arrived, arrived_meta)
    pl.semaphore_wait(barrier, RING - 1 + LAYERS - 1)
    sends = []
    for slot in range(1, EARLY):
        sends += send_block(slot)
    load_precond.wait()
    rhs = rhs_ref[...]
    smooth0 = apply_precond(rhs)
    halo_copies = send_halo(0, smooth0)
    for slot in range(EARLY, RING):
        sends += send_block(slot)

    def multiply(first, count):
        for i in range(count):
            slot = first + i

            @pl.when(slot > 0)
            def _():
                for source, target, out, into in (
                    (stage_meta, arrived_meta, meta_send, meta_recv),
                    (stage, arrived, send_sem, recv_sem),
                ):
                    pltpu.make_async_remote_copy(
                        src_ref=source.at[slot],
                        dst_ref=target.at[slot],
                        send_sem=out.at[slot],
                        recv_sem=into.at[slot],
                        device_id=on_col(after),
                        device_id_type=MESH,
                    ).wait_recv()

            blocks = arrived[slot].reshape(WIDE, BS)
            scaled = blocks.astype(jnp.float32) * arrived_meta[slot, 0:1]
            high = scaled.astype(jnp.bfloat16)
            low = (scaled - high.astype(jnp.float32)).astype(jnp.bfloat16)
            products[i] = lax.dot_general(
                jnp.concatenate([high, low], axis=1),
                jnp.concatenate([blocks, blocks], axis=1),
                (((1,), (1,)), ((), ())),
                preferred_element_type=jnp.float32,
            )

    def row_masks(slot):
        at = jnp.broadcast_to(arrived_meta[slot, 1:2], (8, BS))
        return [jnp.where(at == float(row), 1.0, 0.0) for row in range(ROWS)]

    def accumulate(first, count):
        masks = list(zip(*[row_masks(first + i) for i in range(count)]))

        def add(chunk, inner):
            at = pl.ds(pl.multiple_of(chunk * 8, 8), 8)
            for k in range(3):
                lanes = slice(k * BS, (k + 1) * BS)
                these = [products[i, at, lanes] for i in range(count)]
                for row in range(ROWS):
                    gained = masks[row][0] * these[0]
                    for i in range(1, count):
                        gained += masks[row][i] * these[i]
                    total[row, at, lanes] = total[row, at, lanes] + gained
            return inner

        lax.fori_loop(0, WIDE // 8, add, 0)

    def full_batch(number, carry):
        multiply(number * BATCH, BATCH)
        accumulate(number * BATCH, BATCH)
        return carry

    def correct(slot, i):
        masks = row_masks(slot)
        acc = [jnp.zeros((8, BS), jnp.float32) for _ in range(3)]
        for chunk in range(0, WIDE, 8):
            v = masks[0] * wide[0, chunk : chunk + 8, :]
            for row in range(1, ROWS):
                v += masks[row] * wide[row, chunk : chunk + 8, :]
            for l in range(3):
                acc[l] += products[i, chunk : chunk + 8, l * BS : (l + 1) * BS] * v
        rows_in = lax.broadcasted_iota(jnp.int32, (ROWS, BS), 0).astype(jnp.float32)
        here = rows_in == arrived_meta[slot, 1:2]
        for l in range(3):
            part[0, l] += jnp.where(here, jnp.sum(acc[l], axis=0, keepdims=True), 0.0)

    total[...] = jnp.zeros_like(total)
    lax.fori_loop(0, RING // BATCH // 2, full_batch, 0)
    for copy in halo_copies:
        copy.wait()
    widen(0, slabs)
    lax.fori_loop(RING // BATCH // 2, RING // BATCH - 1, full_batch, 0)
    multiply(RING - 4, 2)
    accumulate(RING - 4, 2)
    apply_normal(0, slabs, True)
    multiply(RING - 2, 2)
    correct(RING - 2, 0)
    correct(RING - 1, 1)
    part_copies = send_part(0)
    inner0 = sum(halo[0, way] * part[0, k] for way, k in slabs)
    inner0 += REGULAR * smooth0 * smooth0
    plane_copies = plane_start(0, [rhs * smooth0, inner0])
    accumulate(RING - 2, 2)

    own_copies = [
        pltpu.make_async_copy(total.at[row, BS : 2 * BS], own_hbm.at[row], out_sem.at[row])
        for row in range(ROWS)
    ]
    for copy in own_copies:
        copy.start()
    slab_copies = []

    def encode(row):
        for way, k, peer in ((1, 2, ahead), (0, 0, before)):
            slab = total[row, k * BS : (k + 1) * BS, :]
            step = jnp.max(jnp.abs(slab), axis=0, keepdims=True) * (1.0 / LEVELS)
            steps[way, row : row + 1, :] = step
            inverse = jnp.where(step > 0.0, 1.0 / step, 0.0)
            scaled = jnp.clip(jnp.round(slab * inverse), -LEVELS, LEVELS)
            codes[way, row] = scaled.astype(jnp.int32).astype(jnp.int16)
            copy = pltpu.make_async_remote_copy(
                src_ref=codes.at[way, row],
                dst_ref=codes_in.at[way, row],
                send_sem=code_send.at[way, row],
                recv_sem=code_recv.at[way, row],
                device_id=on_col(peer),
                device_id_type=MESH,
            )
            copy.start()
            slab_copies.append(copy)

    for row in range(0, 2):
        encode(row)
    for copy in part_copies:
        copy.wait()
    mapped0 = part[0, 1] + part_in[0, 0] + part_in[0, 1] + REGULAR * smooth0
    smooth_mapped = apply_precond(mapped0)
    halo_copies = send_halo(1, smooth_mapped)
    for row in range(2, 4):
        encode(row)
    widen(1, slabs[1:2])
    apply_normal(1, slabs[1:2], True)
    row0 = sum_end(red_p, 0, plane_copies)
    layers_copies = layers_start(0, row0)
    rho_here, curve_here = out_of_lanes(row0, 2)
    guess = jnp.where(curve_here > 0.0, rho_here / curve_here, 0.0)
    near_residual = rhs - guess * mapped0
    near_smooth = smooth0 - guess * smooth_mapped
    for copy in halo_copies:
        copy.wait()
    widen(1, slabs[::2])
    apply_normal(1, slabs[::2], False)
    part_copies = send_part(1)
    moments = [
        near_residual * near_smooth,
        near_residual * smooth_mapped + mapped0 * near_smooth,
        mapped0 * smooth_mapped,
        REGULAR * near_smooth * near_smooth,
        REGULAR * 2.0 * near_smooth * smooth_mapped,
        REGULAR * smooth_mapped * smooth_mapped,
        REGULAR * near_smooth * smooth0,
        REGULAR * smooth_mapped * smooth0,
    ]
    for way, k in slabs:
        other = halo[1, way]
        here = halo[0, way] - guess * other
        near_part = part[0, k] - guess * part[1, k]
        moments[3] += here * near_part
        moments[4] += here * part[1, k] + other * near_part
        moments[5] += other * part[1, k]
        moments[6] += here * part[0, k]
        moments[7] += other * part[0, k]
    plane_copies = plane_start(1, moments)
    for row in range(4, ROWS):
        encode(row)
    for way, peer in ((1, ahead), (0, before)):
        copy = pltpu.make_async_remote_copy(
            src_ref=steps.at[way],
            dst_ref=steps_in.at[way],
            send_sem=step_send.at[way],
            recv_sem=step_recv.at[way],
            device_id=on_col(peer),
            device_id_type=MESH,
        )
        copy.start()
        slab_copies.append(copy)
    rho0, curve0 = out_of_lanes(sum_end(red_z, 0, layers_copies), 2)
    step0 = rho0 / curve0
    rest = step0 - guess
    residual1 = rhs - step0 * mapped0
    smooth1 = smooth0 - step0 * smooth_mapped
    for copy in part_copies:
        copy.wait()
    mapped_smooth = part[1, 1] + part_in[1, 0] + part_in[1, 1] + REGULAR * smooth_mapped
    powers = in_lanes([1.0, -rest, rest * rest, 1.0, -rest, rest * rest, 1.0, -rest])
    row1 = sum_end(red_p, 1, plane_copies) * powers
    layers_copies = layers_start(1, row1)
    for copy in sends:
        copy.wait_send()
    for copy in own_copies:
        copy.wait()
    for copy in slab_copies[:8]:
        copy.wait()
    row1 = sum_end(red_z, 1, layers_copies)
    rho1, curve11, curve10 = (
        jnp.sum(jnp.where((lane >= first) & (lane < last), row1, 0.0), keepdims=True)
        for first, last in ((0, 3), (3, 6), (6, 8))
    )
    ratio = rho1 / rho0
    step1 = rho1 / (curve11 + 2.0 * ratio * curve10 + ratio * ratio * curve0)
    mapped1 = (mapped0 - step0 * mapped_smooth) + ratio * mapped0
    vectors[0] = step0 * smooth0 + step1 * (smooth1 + ratio * smooth0)
    vectors[1] = residual1 - step1 * mapped1
    vectors_copy = pltpu.make_async_copy(vectors, vectors_hbm, load_sem.at[0])
    vectors_copy.start()

    for copy in slab_copies[8:]:
        copy.wait()
    vectors_copy.wait()


def finish(
    codes_hbm,
    steps_hbm,
    own_hbm,
    vectors_hbm,
    normal_hbm,
    x_hbm,
    r_hbm,
    codes,
    steps,
    own,
    vectors,
    normal,
    load_sem,
    small_sem,
    out_sem,
):
    loads = [
        [
            pltpu.make_async_copy(codes_hbm.at[0, row], codes.at[0, row], load_sem.at[0, row]),
            pltpu.make_async_copy(codes_hbm.at[1, row], codes.at[1, row], load_sem.at[1, row]),
            pltpu.make_async_copy(own_hbm.at[row], own.at[row], load_sem.at[2, row]),
        ]
        for row in range(ROWS)
    ]
    load_steps = pltpu.make_async_copy(steps_hbm, steps, small_sem.at[0])
    load_vectors = pltpu.make_async_copy(vectors_hbm, vectors, small_sem.at[1])
    load_steps.start()
    for copies in loads:
        for copy in copies:
            copy.start()
    load_vectors.start()
    rows_in = lax.broadcasted_iota(jnp.int32, (BS, BS), 0)
    columns_in = lax.broadcasted_iota(jnp.int32, (BS, BS), 1)
    diagonal = jnp.where(rows_in == columns_in, REGULAR, 0.0)
    outs = []
    load_steps.wait()
    for row in range(ROWS):
        for copy in loads[row]:
            copy.wait()

        def block(way, l):
            lanes = slice(l * BS, (l + 1) * BS)
            levels = codes[way, row, :, lanes].astype(jnp.int32).astype(jnp.float32)
            return levels * steps[way, row : row + 1, lanes]

        normal[row, 0] = own[row, :, BS : 2 * BS] + diagonal + block(0, 0) + block(1, 2)
        normal[row, 1] = block(0, 1)
        normal[row, 2] = own[row, :, 0:BS]
        normal[row, 3] = own[row, :, 2 * BS :]
        normal[row, 4] = block(1, 1)
        normal[row, 5] = block(0, 2)
        normal[row, 6] = block(1, 0)
        out = pltpu.make_async_copy(normal.at[row], normal_hbm.at[row], out_sem.at[row])
        out.start()
        outs.append(out)
    load_vectors.wait()
    for which, target in enumerate((x_hbm, r_hbm)):
        out = pltpu.make_async_copy(vectors.at[which], target, small_sem.at[2 + which])
        out.start()
        outs.append(out)
    for out in outs:
        out.wait()


def on_device(coeff, scaling, block_rows, precond, rhs):
    f32, bf16 = jnp.float32, jnp.bfloat16
    anywhere = pl.BlockSpec(memory_space=pl.ANY)
    dma = pltpu.SemaphoreType.DMA
    codes, steps, own, vectors = pl.pallas_call(
        kernel,
        out_shape=(
            jax.ShapeDtypeStruct((2, ROWS, BS, WIDE), jnp.int16),
            jax.ShapeDtypeStruct((2, ROWS, WIDE), f32),
            jax.ShapeDtypeStruct((ROWS, BS, WIDE), f32),
            jax.ShapeDtypeStruct((2, ROWS, BS), f32),
        ),
        in_specs=[anywhere] * 5,
        out_specs=(anywhere,) * 4,
        scratch_shapes=[
            pltpu.VMEM((RING, 3, BS, BS), bf16),
            pltpu.SMEM((3, RING), jnp.int32),
            pltpu.VMEM((RING, BS), bf16),
            pltpu.VMEM((ROWS, BS), f32),
            pltpu.VMEM((RING, BS), f32),
            pltpu.VMEM((RING, 3, BS, BS), bf16),
            pltpu.VMEM((RING, 2, BS), f32),
            pltpu.VMEM((RING, 3, BS, BS), bf16),
            pltpu.VMEM((RING, 2, BS), f32),
            pltpu.VMEM((BATCH, WIDE, WIDE), f32),
            pltpu.VMEM((ROWS, WIDE, WIDE), f32),
            pltpu.VMEM((ROWS, BS, BS), f32),
            pltpu.VMEM((ROWS, WIDE, BS), f32),
            pltpu.VMEM((ROWS, BS, BS), f32),
            pltpu.VMEM((2, 3, ROWS, BS), f32),
            pltpu.VMEM((2, 3, ROWS, BS), f32),
            pltpu.VMEM((2, 2, ROWS, BS), f32),
            pltpu.VMEM((2, ROWS, BS, WIDE), jnp.int16),
            pltpu.VMEM((2, ROWS, WIDE), f32),
            pltpu.VMEM((2, ROWS, BS), f32),
            pltpu.VMEM((2, LAYERS, 1, BS), f32),
            pltpu.VMEM((2, RING, 1, BS), f32),
            dma((5,)),
            dma((RING,)),
            dma((RING,)),
            dma((RING,)),
            dma((RING,)),
            dma((2, 3)),
            dma((2, 3)),
            dma((2, 2)),
            dma((2, 2)),
            dma((2, ROWS)),
            dma((2, ROWS)),
            dma((2,)),
            dma((2,)),
            dma((2, LAYERS + RING)),
            dma((2, LAYERS + RING)),
            dma((ROWS,)),
        ],
        compiler_params=pltpu.CompilerParams(
            collective_id=0, has_side_effects=True, vmem_limit_bytes=56 << 20
        ),
    )(coeff, scaling, block_rows.T, precond, rhs)
    return pl.pallas_call(
        finish,
        out_shape=(
            jax.ShapeDtypeStruct((ROWS, 7, BS, BS), f32),
            jax.ShapeDtypeStruct((ROWS, BS), f32),
            jax.ShapeDtypeStruct((ROWS, BS), f32),
        ),
        in_specs=[anywhere] * 4,
        out_specs=(anywhere,) * 3,
        scratch_shapes=[
            pltpu.VMEM((2, ROWS, BS, WIDE), jnp.int16),
            pltpu.VMEM((2, ROWS, WIDE), f32),
            pltpu.VMEM((ROWS, BS, WIDE), f32),
            pltpu.VMEM((2, ROWS, BS), f32),
            pltpu.VMEM((ROWS, 7, BS, BS), f32),
            dma((3, ROWS)),
            dma((4,)),
            dma((ROWS,)),
        ],
        compiler_params=pltpu.CompilerParams(vmem_limit_bytes=56 << 20),
    )(codes, steps, own, vectors)


def solution(mesh):
    whole = P(("grp", "col"))
    return jax.shard_map(
        on_device,
        mesh=mesh,
        in_specs=(whole,) * 5,
        out_specs=(whole,) * 3,
        check_vma=False,
    )
```
